32 devices in a mesh: grp: 2 (over y), row: 4 (over z), col: 4 (over x, core).
Axes of the slice: x: 2, y: 2, z: 4, core: 2. Of those that a mesh axis runs over, the one named last changes fastest.
Arguments:
- sky_cube: bfloat16 [1024, 512, 512], P(('grp', 'row'), 'col'), parts along dimension 0, may hold values from -40 to 40
- half_widths: int32 [512], replicated, may hold values from 1 to 16, as said below
- pixel_mask: int32 [1024, 512], P(('grp', 'row'), 'col'), parts along dimension 0, may hold values 0 or 1
- foreground_modes: float32 [32, 512], P('grp'), parts along dimension 0, may hold values from -6 to 6
Outputs:
- spectrum: float32 [512, 2, 512, 512], P(('grp', 'row', 'col')), parts along dimension 0
- channel_weights: float32 [1024], P('grp'), parts along dimension 0
The draws below stay inside these ranges and needn't reach their ends.
There are 2 independent parts, one for each index of `grp`. The reference program is written for one: setup_inputs(seed, part) draws one part's arguments, and reference() takes and returns one part's arrays. A program takes and returns all parts, laid end to end along the dimension named above; an argument that names none is the same for every part. Nothing has to cross between parts.
Inputs may be any that keep to these rules, and one draw needn't show every extreme that they name: `half_widths`: some channel has half-width exactly 16 and some exactly 1.
All inputs are finite; a program needn't handle non-finite values. No bound on the sum of `pixel_mask` on one device may be relied on, other than what follows from the above.
Results may differ from the reference program's by a relative error of at most 0.0087.
Values may be sent and summed in bfloat16 or wider, within the bound.
No kernel may reach another device: no remote copies, remote signals or barrier semaphores. Data moves between devices by JAX's collectives and lax.ppermute only.
A program may use at most 192 MiB of HBM per device.

```python
import math
import jax
import jax.numpy as jnp
from jax import lax

NR = 512
NC = 512
NF = 512
NMODE = 16
HALF = 16


def sky_modes(key):
    mode_key = jax.random.fold_in(key, 11)
    drawn = jax.random.normal(mode_key, (NMODE, NF), jnp.float32)
    return jnp.clip(drawn, -6.0, 6.0)


def draw_foreground_modes(key, part):
    return sky_modes(key)


def diffuse_field(key, row_place, col_place):
    wave_count = 6
    length_key = jax.random.fold_in(key, 31)
    turn_key = jax.random.fold_in(key, 32)
    phase_key = jax.random.fold_in(key, 33)
    strength_key = jax.random.fold_in(key, 34)
    lengths = jnp.exp(jax.random.uniform(length_key, (wave_count, NMODE), jnp.float32, math.log(12.0), math.log(96.0)))
    turns = jax.random.uniform(turn_key, (wave_count, NMODE), jnp.float32, 0.0, 2.0 * math.pi)
    phases = jax.random.uniform(phase_key, (wave_count, NMODE), jnp.float32, 0.0, 2.0 * math.pi)
    strengths = jax.random.normal(strength_key, (wave_count, NMODE), jnp.float32) * 0.03
    field = jnp.zeros((NR, NC, NMODE), jnp.float32)
    for wave_index in range(wave_count):
        along_rows = 2.0 * math.pi * jnp.cos(turns[wave_index]) / lengths[wave_index]
        along_cols = 2.0 * math.pi * jnp.sin(turns[wave_index]) / lengths[wave_index]
        angle_field = row_place * along_rows + col_place * along_cols + phases[wave_index]
        field = field + strengths[wave_index] * jnp.cos(angle_field)
    return field


def compact_sources(key, row_place, col_place):
    source_count = 16
    centre_rows = jax.random.randint(jax.random.fold_in(key, 41), (source_count,), 0, NR).astype(jnp.float32)
    centre_cols = jax.random.randint(jax.random.fold_in(key, 42), (source_count,), 0, NC).astype(jnp.float32)
    source_widths = jnp.exp(jax.random.uniform(jax.random.fold_in(key, 43), (source_count,), jnp.float32, math.log(0.8), math.log(2.0)))
    brightness = jnp.exp(jax.random.uniform(jax.random.fold_in(key, 44), (source_count,), jnp.float32, math.log(8.0), math.log(30.0)))
    coefficients = jax.random.normal(jax.random.fold_in(key, 45), (source_count, NMODE), jnp.float32) / math.sqrt(NMODE)
    row_gap = row_place - centre_rows
    col_gap = col_place - centre_cols
    profile = jnp.exp(-(row_gap * row_gap + col_gap * col_gap) / (2.0 * source_widths * source_widths)) * brightness
    return jnp.einsum('rcs,sk->rck', profile, coefficients)


def draw_sky_cube(key, part):
    modes_drawn = sky_modes(key)
    noise_key = jax.random.fold_in(key, 22)
    sigma_key = jax.random.fold_in(key, 23)
    scale_key = jax.random.fold_in(key, 24)
    row_place = jnp.arange(NR, dtype=jnp.int32).astype(jnp.float32)[:, None, None]
    col_place = jnp.arange(NC, dtype=jnp.int32).astype(jnp.float32)[None, :, None]
    amplitudes = diffuse_field(key, row_place, col_place) + compact_sources(key, row_place, col_place)
    noise_field = jax.random.normal(noise_key, (NR, NC, NF), jnp.float32)
    channel_sigma = jnp.exp(jax.random.uniform(sigma_key, (NF,), jnp.float32, math.log(0.03), math.log(0.3)))
    pixel_scale = jnp.exp(jax.random.uniform(scale_key, (NR, NC, 1), jnp.float32, math.log(0.3), math.log(3.0)))
    position = jnp.arange(NR, dtype=jnp.int32).astype(jnp.float32) / NR - 0.5
    row_rise = (3.0 ** position)[:, None, None]
    foreground = jnp.einsum('rck,kf->rcf', amplitudes, modes_drawn)
    values = row_rise * (foreground + channel_sigma[None, None, :] * pixel_scale * noise_field)
    return jnp.clip(values, -40.0, 40.0).astype(jnp.bfloat16)


def draw_half_widths(key, part):
    drawn = jax.random.randint(jax.random.fold_in(key, 3), (NF,), 1, HALF + 1)
    widest = jax.random.randint(jax.random.fold_in(key, 4), (), 0, NF)
    drawn = drawn.at[widest].set(HALF)
    drawn = drawn.at[(widest + 1) % NF].set(1)
    return drawn.astype(jnp.int32)


def set_ends(array, own_key, smallest, high):
    longest = array.shape.index(max(array.shape))
    spots = []
    for shift in (0, 1):
        where = [jax.random.randint(jax.random.fold_in(own_key, axis), (), 0, length) for axis, length in enumerate(array.shape)]
        where[longest] = (where[longest] + shift) % array.shape[longest]
        spots.append(tuple(where))
    return array.at[spots[0]].set(smallest).at[spots[1]].set(high)


def setup_inputs(seed: int = 0, part: int = 0) -> dict:
    arg_keys = jax.random.split(jax.random.key(seed), 5)
    own_keys = jax.random.split(jax.random.fold_in(arg_keys[4], part), 5)
    sky_cube = draw_sky_cube(jax.random.fold_in(jax.random.fold_in(arg_keys[4], part), 71), part)
    half_widths = draw_half_widths(jax.random.fold_in(arg_keys[4], 71), part)
    pixel_mask = set_ends((jax.random.randint(own_keys[2], (NR, NC), 0, 4) < 3).astype(jnp.int32), jax.random.fold_in(own_keys[2], 1), 0, 1)
    foreground_modes = draw_foreground_modes(jax.random.fold_in(jax.random.fold_in(arg_keys[4], part), 71), part)
    return dict(sky_cube=sky_cube, half_widths=half_widths, pixel_mask=pixel_mask, foreground_modes=foreground_modes)


highest = lax.Precision.HIGHEST

def make_taps(half_widths):
    offsets = jnp.arange(2 * HALF + 1, dtype=jnp.int32) - HALF
    distance = offsets.astype(jnp.float32)[:, None]
    spread = half_widths.astype(jnp.float32)[None, :] * 0.5
    inside = jnp.abs(offsets)[:, None] <= half_widths[None, :]
    profile = jnp.where(inside, jnp.exp(-distance * distance / (2.0 * spread * spread)), jnp.float32(0.0))
    return (profile / lax.optimization_barrier(jnp.sum(profile, axis=0, keepdims=True))).astype(jnp.bfloat16)

def window_taper(length):
    angles = 2.0 * math.pi * jnp.arange(length, dtype=jnp.int32).astype(jnp.float32) / (length - 1)
    return 0.35875 - 0.48829 * jnp.cos(angles) + 0.14128 * jnp.cos(2.0 * angles) - 0.01168 * jnp.cos(3.0 * angles)

def dft_table(length):
    indices = jnp.arange(length, dtype=jnp.int32)
    product = indices[:, None] * indices[None, :] % length
    angles = 2.0 * math.pi * product.astype(jnp.float32) / length
    cosine = jnp.cos(angles) / math.sqrt(length)
    sine_part = -jnp.sin(angles) / math.sqrt(length)
    table = jnp.stack([jnp.stack([cosine, -sine_part]), jnp.stack([sine_part, cosine])])
    return table.astype(jnp.bfloat16)

def delay_table():
    channel_index = jnp.arange(NF, dtype=jnp.int32)
    delay_index = jnp.arange(NF // 2, dtype=jnp.int32)
    product = channel_index[:, None] * delay_index[None, :] % NF
    angles = 2.0 * math.pi * product.astype(jnp.float32) / NF
    scale = window_taper(NF)[:, None] / math.sqrt(NF)
    return jnp.stack([jnp.cos(angles) * scale, -jnp.sin(angles) * scale], axis=1).reshape(NF, NF)

def smooth_axis(data, beam_taps, axis):
    length = data.shape[axis]
    widths = [(0, 0), (0, 0), (0, 0)]
    widths[axis] = (HALF, HALF)
    padded = jnp.pad(data, widths)
    taps_wide = beam_taps.astype(jnp.float32)

    def add_tap(tap, running):
        piece = lax.dynamic_slice_in_dim(padded, tap, length, axis)
        return running + taps_wide[tap][None, None, :] * piece
    return lax.fori_loop(0, 2 * HALF + 1, add_tap, jnp.zeros(data.shape, jnp.float32))

def spatial_transform(delay_slab):
    column_table = dft_table(NC).astype(jnp.float32)
    row_table = dft_table(NR).astype(jnp.float32)
    halfway = jnp.einsum('kmrc,nmcd->knrd', delay_slab.astype(jnp.float32), column_table, precision=highest)
    halfway = lax.optimization_barrier(halfway.astype(jnp.bfloat16)).astype(jnp.float32)
    return jnp.einsum('nmsr,kmrd->knsd', row_table, halfway, precision=highest)

def reference(sky_cube, half_widths, pixel_mask, foreground_modes):
    beam_taps = make_taps(half_widths)
    row_smoothed = smooth_axis(sky_cube.astype(jnp.float32), beam_taps, 0).astype(jnp.bfloat16)
    row_smoothed = lax.optimization_barrier(row_smoothed).astype(jnp.float32)
    smoothed = smooth_axis(row_smoothed, beam_taps, 1)
    masked = pixel_mask.astype(jnp.float32)[:, :, None] * smoothed
    power_sum = lax.optimization_barrier(jnp.sum(masked * masked, axis=(0, 1)))
    weights = 1.0 / (power_sum / (NR * NC) + 1e-05)
    channel_weights = weights / jnp.mean(weights)
    weighted_modes = foreground_modes * weights[None, :]
    normal_matrix = jnp.dot(weighted_modes.astype(jnp.float32), foreground_modes.T.astype(jnp.float32), precision=highest, preferred_element_type=jnp.float32)
    pixels = masked.reshape(NR * NC, NF)
    projected = jnp.dot(pixels.astype(jnp.float32), weighted_modes.T.astype(jnp.float32), precision=highest, preferred_element_type=jnp.float32)
    factor = jnp.linalg.cholesky(normal_matrix)
    amplitude = jax.scipy.linalg.cho_solve((factor, True), projected.T)
    cleaned = pixels - jnp.dot(amplitude.T.astype(jnp.float32), foreground_modes.astype(jnp.float32), precision=highest, preferred_element_type=jnp.float32)
    delays = jnp.dot(cleaned.astype(jnp.float32), delay_table().astype(jnp.float32), precision=highest, preferred_element_type=jnp.float32).astype(jnp.bfloat16)
    delay_cube = delays.reshape(NR, NC, 2, NF // 2).transpose(3, 2, 0, 1)

    def one_delay(delay_slab):
        return spatial_transform(delay_slab[None])[0]
    spectrum = lax.map(one_delay, delay_cube)
    return (spectrum, channel_weights)
```

```python
import functools
import math

import jax
import jax.numpy as jnp
import numpy as np
from jax import lax
from jax.experimental import pallas as pl
from jax.experimental.pallas import tpu as pltpu
from jax.sharding import PartitionSpec as P

HALF = 16
VMEM_LIMIT = 48 * 1024 * 1024
CHUNKS = 4

highest = lax.Precision.HIGHEST


def padded(x, sides, width):
    for axis, dim in sides:
        size, length = (lax.axis_size(axis), x.shape[dim])
        up = [(i, (i + 1) % size) for i in range(size - 1)]
        down = [(j, i) for i, j in up]
        last = lax.slice_in_dim(x, length - width, length, axis=dim)
        initial = lax.slice_in_dim(x, 0, width, axis=dim)
        before = lax.ppermute(last, axis, up)
        after = lax.ppermute(initial, axis, down)
        x = jnp.concatenate([before, x, after], axis=dim)
    return x


def make_taps(half_widths):
    offsets = jnp.arange(2 * HALF + 1, dtype=jnp.int32) - HALF
    distance = offsets.astype(jnp.float32)[:, None]
    spread = half_widths.astype(jnp.float32)[None, :] * 0.5
    inside = jnp.abs(offsets)[:, None] <= half_widths[None, :]
    profile = jnp.where(
        inside, jnp.exp(-distance * distance / (2.0 * spread * spread)), jnp.float32(0.0)
    )
    return (profile / jnp.sum(profile, axis=0, keepdims=True)).astype(jnp.bfloat16)


def banded_taps(outputs, beam_taps):
    offsets = (
        jnp.arange(outputs + 2 * HALF, dtype=jnp.int32)[None, :]
        - jnp.arange(outputs, dtype=jnp.int32)[:, None]
    )
    one_hot = (
        offsets[:, :, None] == jnp.arange(2 * HALF + 1, dtype=jnp.int32)[None, None, :]
    ).astype(jnp.bfloat16)
    return jnp.einsum("oit,tf->oif", one_hot, beam_taps, preferred_element_type=jnp.float32).astype(
        jnp.bfloat16
    )


def window_taper(length):
    angles = 2.0 * math.pi * np.arange(length) / (length - 1)
    return (
        0.35875
        - 0.48829 * np.cos(angles)
        + 0.14128 * np.cos(2.0 * angles)
        - 0.01168 * np.cos(3.0 * angles)
    )


def dft_parts(length):
    indices = np.arange(length)
    angles = 2.0 * math.pi * (indices[:, None] * indices[None, :] % length) / length
    scale = 1.0 / math.sqrt(length)
    return (
        (np.cos(angles) * scale).astype(jnp.bfloat16),
        (-np.sin(angles) * scale).astype(jnp.bfloat16),
    )


def delay_rows(channels, peers, sizes):
    per_device = channels // 2 // peers
    order, start = [], 0
    for size in sizes:
        for peer in range(peers):
            order.extend(peer * per_device + start + item for item in range(size))
        start += size
    delays = np.asarray(order)
    channel = np.arange(channels)
    angles = 2.0 * math.pi * (delays[:, None] * channel[None, :] % channels) / channels
    rows = np.stack([np.cos(angles), -np.sin(angles)], axis=1).reshape(channels, channels)
    return (rows * (window_taper(channels) / math.sqrt(channels))[None, :]).astype(np.float32)


def tap_table():
    distance = np.arange(HALF + 1, dtype=np.float32)
    table = np.zeros((HALF, HALF + 1), np.float32)
    for width in range(1, HALF + 1):
        spread = np.float32(width) * np.float32(0.5)
        profile = np.exp(-distance * distance / (np.float32(2.0) * spread * spread))
        profile = np.where(distance <= width, profile, np.float32(0.0)).astype(np.float32)
        total = profile[0] + np.float32(2.0) * np.sum(profile[1:], dtype=np.float32)
        table[width - 1] = profile / total
    return table


def band_table(out_places, in_places):
    taps = np.concatenate([tap_table(), np.zeros((HALF, 1), np.float32)], axis=1)
    distance = np.abs(np.asarray(out_places)[:, None] - np.asarray(in_places)[None, :])
    return taps[:, np.minimum(distance, HALF + 1)].astype(jnp.bfloat16)


def smooth_kernel(row_pieces, side_pieces, widths, mask, row_band, side_band, col_band, *refs):
    rows, sides = refs[:row_pieces], refs[row_pieces : row_pieces + side_pieces]
    high, low, power, staged = refs[row_pieces + side_pieces :]
    block = rows[0].shape[0]
    outputs, columns = mask.shape
    first = pl.program_id(0) * block
    kept = mask[...]
    for j in range(block):
        width = widths[first + j] - 1
        data = jnp.concatenate([piece[j] for piece in rows], axis=0)
        side = jnp.concatenate([piece[j] for piece in sides], axis=1)
        centre = jnp.dot(row_band[width], data, preferred_element_type=jnp.float32)
        edge = jnp.dot(side, side_band[width], preferred_element_type=jnp.float32)
        smoothed_rows = jnp.concatenate(
            [centre.astype(jnp.bfloat16), edge.T.astype(jnp.bfloat16)], axis=1
        )
        smoothed = jnp.dot(smoothed_rows, col_band[width], preferred_element_type=jnp.float32)
        staged[pl.ds(j, outputs, stride=block), :] = smoothed * kept

    group = 8

    def split(step, total):
        start = pl.multiple_of(step * group, group)
        value = staged[pl.ds(pl.multiple_of(start * block, group * block), group * block), :]
        rounded = value.astype(jnp.bfloat16)
        rest = (value - rounded.astype(jnp.float32)).astype(jnp.bfloat16)
        high[pl.ds(start, group)] = rounded.reshape(group, block, columns)
        low[pl.ds(start, group)] = rest.reshape(group, block, columns)
        return total + jnp.sum((value * value).reshape(group, block, columns), axis=0)

    power[...] = lax.fori_loop(
        0, outputs // group, split, jnp.zeros((block, columns), jnp.float32)
    )


def smooth(half_widths, mask, rows, sides, tables, block=16):
    channels, _, columns = rows[0].shape
    outputs = mask.shape[0]
    whole = lambda shape: pl.BlockSpec(shape, lambda i: (0,) * len(shape))
    piece = lambda x: pl.BlockSpec((block,) + x.shape[1:], lambda i: (i, 0, 0))
    split_spec = pl.BlockSpec((outputs, block, columns), lambda i: (0, i, 0))
    split_shape = jax.ShapeDtypeStruct((outputs, channels, columns), jnp.bfloat16)
    return pl.pallas_call(
        functools.partial(smooth_kernel, len(rows), len(sides)),
        grid=(channels // block,),
        in_specs=[pl.BlockSpec(memory_space=pltpu.SMEM), whole(mask.shape)]
        + [whole(t.shape) for t in tables]
        + [piece(x) for x in rows + sides],
        out_specs=[split_spec, split_spec, pl.BlockSpec((block, columns), lambda i: (i, 0))],
        out_shape=[
            split_shape,
            split_shape,
            jax.ShapeDtypeStruct((channels, columns), jnp.float32),
        ],
        scratch_shapes=[pltpu.VMEM((outputs * block, columns), jnp.float32)],
        compiler_params=pltpu.CompilerParams(vmem_limit_bytes=VMEM_LIMIT),
        cost_estimate=pl.CostEstimate(
            flops=4 * channels * outputs * columns * 160, bytes_accessed=80_000_000, transcendentals=0
        ),
        name="smooth",
    )(half_widths, mask, *tables, *rows, *sides)


def delay_kernel(modes, high, low, out, staged):
    rows = high.shape[0]
    count, _, columns = out.shape
    for pair in range(rows // 2):
        first, second = 2 * pair, 2 * pair + 1
        coarse = jnp.concatenate([high[first], high[second]], axis=1)
        fine = jnp.concatenate([low[first], low[second]], axis=1)
        both = jnp.dot(modes[...], coarse, preferred_element_type=jnp.float32)
        value = both[:count] + both[count:]
        value = value + jnp.dot(modes[:count], fine, preferred_element_type=jnp.float32)
        staged[pl.ds(first, count, stride=rows), :] = value[:, :columns]
        staged[pl.ds(second, count, stride=rows), :] = value[:, columns:]
    out[...] = staged[...].reshape(count, rows, columns).astype(jnp.bfloat16)


def delay_chunk(matrix, high, low, block=16):
    tile_rows, channels, columns = high.shape
    count = matrix.shape[0] // 2
    spec = pl.BlockSpec((block, channels, columns), lambda i: (i, 0, 0))
    return pl.pallas_call(
        delay_kernel,
        grid=(tile_rows // block,),
        in_specs=[pl.BlockSpec(matrix.shape, lambda i: (0, 0)), spec, spec],
        out_specs=pl.BlockSpec((count, block, columns), lambda i: (0, i, 0)),
        out_shape=jax.ShapeDtypeStruct((count, tile_rows, columns), jnp.bfloat16),
        scratch_shapes=[pltpu.VMEM((count * block, columns), jnp.float32)],
        compiler_params=pltpu.CompilerParams(vmem_limit_bytes=VMEM_LIMIT),
        cost_estimate=pl.CostEstimate(
            flops=6 * count * channels * tile_rows * columns,
            bytes_accessed=40_000_000,
            transcendentals=0,
        ),
        name="delays",
    )(matrix, high, low)


def spatial_kernel(row_count, col_count, has_previous, slab, col_table, row_table, *refs):
    out, halfway = refs[-2:]
    _, _, tile_rows, _ = slab.shape
    side = row_count * tile_rows
    for a in range(row_count):
        line = jnp.concatenate(
            [slab[a * col_count + b, k] for k in range(2) for b in range(col_count)], axis=1
        )
        part = jnp.dot(line, col_table[...], preferred_element_type=jnp.float32)
        part = part.astype(jnp.bfloat16)
        columns = part.shape[1] // 2
        halfway[pl.ds(a * tile_rows, tile_rows), :] = part[:, :columns]
        halfway[pl.ds(side + a * tile_rows, tile_rows), :] = part[:, columns:]
    step = side // 2
    for k in range(2):
        for s in range(side // step):
            rows = row_table[pl.ds(k * side + s * step, step), :]
            out[0, k, pl.ds(s * step, step), :] = jnp.dot(
                rows, halfway[...], preferred_element_type=jnp.float32
            )


def spatial_chunk(received, col_table, row_table, shape, start, previous):
    peers, parts, tile_rows, tile_cols = received.shape
    items = parts // 2
    side, columns = shape[2], shape[3]
    in_specs = [
        pl.BlockSpec((peers, 2, tile_rows, tile_cols), lambda i: (0, i, 0, 0)),
        pl.BlockSpec(col_table.shape, lambda i: (0, 0)),
        pl.BlockSpec(row_table.shape, lambda i: (0, 0)),
    ]
    operands = [received, col_table, row_table]
    aliases = {}
    if previous is not None:
        in_specs.append(pl.BlockSpec(memory_space=pl.ANY))
        operands.append(previous)
        aliases = {3: 0}
    return pl.pallas_call(
        functools.partial(
            spatial_kernel, side // tile_rows, columns // tile_cols, previous is not None
        ),
        grid=(items,),
        in_specs=in_specs,
        out_specs=pl.BlockSpec((1, 2, side, columns), lambda i: (start + i, 0, 0, 0)),
        out_shape=jax.ShapeDtypeStruct(shape, jnp.float32),
        scratch_shapes=[pltpu.VMEM((2 * side, columns), jnp.bfloat16)],
        input_output_aliases=aliases,
        compiler_params=pltpu.CompilerParams(vmem_limit_bytes=VMEM_LIMIT),
        cost_estimate=pl.CostEstimate(
            flops=16 * items * side * side * columns,
            bytes_accessed=items * 12 * side * columns,
            transcendentals=0,
        ),
        name="spatial",
    )(*operands)


def shifted(x, steps):
    axes = tuple(axis for axis, _ in steps)
    sizes = [lax.axis_size(axis) for axis in axes]
    pairs = []
    for place in np.ndindex(*sizes):
        target = [p + s for p, (_, s) in zip(place, steps)]
        if all(0 <= t < n for t, n in zip(target, sizes)):
            pairs.append(
                (int(np.ravel_multi_index(place, sizes)), int(np.ravel_multi_index(target, sizes)))
            )
    return lax.ppermute(x, axes if len(axes) > 1 else axes[0], pairs)


def split_high_low(x):
    rounded = x.astype(jnp.bfloat16)
    return rounded, (x - rounded.astype(jnp.float32)).astype(jnp.bfloat16)


def tiled_body(sky_cube, half_widths, pixel_mask, foreground_modes):
    tile_rows, tile_cols, channels = sky_cube.shape
    row_count, col_count = lax.axis_size("row"), lax.axis_size("col")
    peers = row_count * col_count
    per_device = channels // 2 // peers
    sides, columns = row_count * tile_rows, col_count * tile_cols

    top = shifted(sky_cube[-HALF:], (("row", 1),))
    bottom = shifted(sky_cube[:HALF], (("row", -1),))
    left = shifted(sky_cube[:, -HALF:], (("col", 1),))
    right = shifted(sky_cube[:, :HALF], (("col", -1),))
    corners = [
        [
            shifted(
                sky_cube[(slice(-HALF, None) if v > 0 else slice(0, HALF))][
                    :, (slice(-HALF, None) if h > 0 else slice(0, HALF))
                ],
                (("row", v), ("col", h)),
            )
            for h in (1, -1)
        ]
        for v in (1, -1)
    ]
    centre_t = jnp.transpose(sky_cube, (2, 0, 1))
    caps_t = jnp.transpose(jnp.concatenate([top, bottom], axis=0), (2, 0, 1))
    flank_t = jnp.transpose(jnp.concatenate([left, right], axis=1), (2, 1, 0))
    corner = jnp.concatenate([jnp.concatenate(line, axis=1) for line in corners], axis=0)
    corner_t = jnp.transpose(corner, (2, 1, 0))

    def places(length):
        return list(range(length)) + list(range(-HALF, 0)) + list(range(length, length + HALF))

    out_rows = list(range(tile_rows))
    row_band = band_table(out_rows, places(tile_rows))
    side_band = np.swapaxes(row_band, 1, 2)
    col_band = np.swapaxes(band_table(list(range(tile_cols)), places(tile_cols)), 1, 2)
    high, low, power = smooth(
        half_widths,
        pixel_mask.astype(jnp.float32),
        [centre_t, caps_t],
        [flank_t, corner_t],
        [row_band, side_band, col_band],
    )

    chunks = math.gcd(CHUNKS, per_device)
    sizes = [per_device // chunks] * chunks
    delay_table = delay_rows(channels, peers, sizes)
    mode_delays = jnp.dot(
        delay_table, foreground_modes.T, precision=highest, preferred_element_type=jnp.float32
    )
    power_sum = lax.psum(jnp.sum(power, axis=1), ("row", "col"))
    weights = 1.0 / (power_sum / (sides * columns) + 1e-05)
    channel_weights = weights / jnp.mean(weights)
    weighted_modes = foreground_modes * weights[None, :]
    normal_matrix = jnp.dot(
        weighted_modes, foreground_modes.T, precision=highest, preferred_element_type=jnp.float32
    )
    factor = jnp.linalg.cholesky(normal_matrix)
    solved = jax.scipy.linalg.cho_solve((factor, True), weighted_modes)
    matrix = delay_table - jnp.dot(
        mode_delays, solved, precision=highest, preferred_element_type=jnp.float32
    )
    matrix_high, matrix_low = split_high_low(matrix)

    cos_c, sin_c = dft_parts(columns)
    col_table = np.block([[cos_c, sin_c], [-sin_c, cos_c]])
    cos_r, sin_r = dft_parts(sides)
    row_table = np.block([[cos_r, -sin_r], [sin_r, cos_r]])

    spectrum = None
    start = 0
    for size in sizes:
        begin, count = 2 * start * peers, 2 * size * peers
        both = jnp.concatenate(
            [matrix_high[begin : begin + count], matrix_low[begin : begin + count]], axis=0
        )
        delays = delay_chunk(both, high, low)
        delays = delays.reshape(peers, 2 * size, tile_rows, tile_cols)
        received = lax.all_to_all(delays, ("row", "col"), split_axis=0, concat_axis=0, tiled=True)
        spectrum = spatial_chunk(
            received, col_table, row_table, (per_device, 2, sides, columns), start, spectrum
        )
        start += size
    return (spectrum, channel_weights)


def small_tile_body(sky_cube, half_widths, pixel_mask, foreground_modes):
    tile_rows, tile_cols, channels = sky_cube.shape
    row_count, col_count = lax.axis_size("row"), lax.axis_size("col")
    peers = row_count * col_count
    per_device = channels // 2 // peers
    sides, columns = row_count * tile_rows, col_count * tile_cols
    beam_taps = make_taps(half_widths)
    extended = padded(sky_cube, (("row", 0),), HALF)
    row_part = jnp.einsum(
        "oif,icf->ocf",
        banded_taps(tile_rows, beam_taps),
        extended,
        preferred_element_type=jnp.float32,
    ).astype(jnp.bfloat16)
    row_smoothed = padded(row_part, (("col", 1),), HALF)
    smoothed = jnp.einsum(
        "oif,rif->rof",
        banded_taps(tile_cols, beam_taps),
        row_smoothed,
        preferred_element_type=jnp.float32,
    )
    masked = pixel_mask.astype(jnp.float32)[:, :, None] * smoothed
    pixels = masked.reshape(tile_rows * tile_cols, channels)
    power_sum = lax.psum(jnp.sum(masked * masked, axis=(0, 1)), ("row", "col"))
    weights = 1.0 / (power_sum / (sides * columns) + 1e-05)
    channel_weights = weights / jnp.mean(weights)
    weighted_modes = foreground_modes * weights[None, :]
    normal_matrix = jnp.dot(
        weighted_modes, foreground_modes.T, precision=highest, preferred_element_type=jnp.float32
    )
    projected = jnp.dot(
        pixels, weighted_modes.T, precision=highest, preferred_element_type=jnp.float32
    )
    factor = jnp.linalg.cholesky(normal_matrix)
    amplitude = jax.scipy.linalg.cho_solve((factor, True), projected.T)
    cleaned = pixels - jnp.dot(
        amplitude.T, foreground_modes, precision=highest, preferred_element_type=jnp.float32
    )
    delay_tile = lax.dot_general(
        delay_rows(channels, peers, [per_device]),
        cleaned,
        (((1,), (1,)), ((), ())),
        precision=highest,
        preferred_element_type=jnp.float32,
    )
    sendable = delay_tile.astype(jnp.bfloat16).reshape(
        peers, per_device, 2, tile_rows, tile_cols
    )
    regrouped = lax.all_to_all(sendable, ("row", "col"), split_axis=0, concat_axis=0, tiled=True)
    slab = regrouped.reshape(row_count, col_count, per_device, 2, tile_rows, tile_cols)
    slab = slab.transpose(2, 3, 0, 4, 1, 5).reshape(per_device, 2, sides, columns)
    cos_c, sin_c = dft_parts(columns)
    col_table = np.stack([np.stack([cos_c, -sin_c]), np.stack([sin_c, cos_c])])
    cos_r, sin_r = dft_parts(sides)
    row_table = np.stack([np.stack([cos_r, -sin_r]), np.stack([sin_r, cos_r])])
    halfway = jnp.einsum(
        "kmrc,nmcd->knrd", slab, col_table, preferred_element_type=jnp.float32
    ).astype(jnp.bfloat16)
    spectrum = jnp.einsum(
        "nmsr,kmrd->knsd", row_table, halfway, preferred_element_type=jnp.float32
    )
    return (spectrum, channel_weights)


def body(sky_cube, half_widths, pixel_mask, foreground_modes):
    tile_rows, tile_cols, channels = sky_cube.shape
    fits = tile_rows % 128 == 0 and tile_cols % 128 == 0 and channels % 128 == 0
    run = tiled_body if fits else small_tile_body
    return run(sky_cube, half_widths, pixel_mask, foreground_modes)


def solution(mesh):
    return jax.shard_map(
        body,
        mesh=mesh,
        in_specs=(P(("grp", "row"), "col", None), P(), P(("grp", "row"), "col"), P("grp", None)),
        out_specs=(P(("grp", "row", "col"), None, None, None), P("grp")),
        check_vma=False,
    )
```

```python
import functools
import math

import jax
import jax.numpy as jnp
import numpy as np
from jax import lax
from jax.experimental import pallas as pl
from jax.experimental.layout import Layout, with_layout_constraint
from jax.experimental.pallas import tpu as pltpu
from jax.sharding import PartitionSpec as P

HALF = 16
VMEM_LIMIT = 48 * 1024 * 1024
PACK = 4
FIRST, LAST = slice(0, HALF), slice(-HALF, None)
END_DELAYS = 2

highest = lax.Precision.HIGHEST


def padded(x, sides, width):
    for axis, dim in sides:
        size, length = (lax.axis_size(axis), x.shape[dim])
        up = [(i, (i + 1) % size) for i in range(size - 1)]
        down = [(j, i) for i, j in up]
        last = lax.slice_in_dim(x, length - width, length, axis=dim)
        initial = lax.slice_in_dim(x, 0, width, axis=dim)
        before = lax.ppermute(last, axis, up)
        after = lax.ppermute(initial, axis, down)
        x = jnp.concatenate([before, x, after], axis=dim)
    return x


def make_taps(half_widths):
    offsets = jnp.arange(2 * HALF + 1, dtype=jnp.int32) - HALF
    distance = offsets.astype(jnp.float32)[:, None]
    spread = half_widths.astype(jnp.float32)[None, :] * 0.5
    inside = jnp.abs(offsets)[:, None] <= half_widths[None, :]
    profile = jnp.where(
        inside, jnp.exp(-distance * distance / (2.0 * spread * spread)), jnp.float32(0.0)
    )
    return (profile / jnp.sum(profile, axis=0, keepdims=True)).astype(jnp.bfloat16)


def banded_taps(outputs, beam_taps):
    offsets = (
        jnp.arange(outputs + 2 * HALF, dtype=jnp.int32)[None, :]
        - jnp.arange(outputs, dtype=jnp.int32)[:, None]
    )
    one_hot = (
        offsets[:, :, None] == jnp.arange(2 * HALF + 1, dtype=jnp.int32)[None, None, :]
    ).astype(jnp.bfloat16)
    return jnp.einsum("oit,tf->oif", one_hot, beam_taps, preferred_element_type=jnp.float32).astype(
        jnp.bfloat16
    )


def window_taper(length):
    angles = 2.0 * math.pi * np.arange(length) / (length - 1)
    return (
        0.35875
        - 0.48829 * np.cos(angles)
        + 0.14128 * np.cos(2.0 * angles)
        - 0.01168 * np.cos(3.0 * angles)
    )


def dft_parts(length):
    indices = np.arange(length)
    angles = 2.0 * math.pi * (indices[:, None] * indices[None, :] % length) / length
    scale = 1.0 / math.sqrt(length)
    return (
        (np.cos(angles) * scale).astype(jnp.bfloat16),
        (-np.sin(angles) * scale).astype(jnp.bfloat16),
    )


def delay_rows(channels, peers, sizes):
    per_device = channels // 2 // peers
    order, start = [], 0
    for size in sizes:
        for peer in range(peers):
            order.extend(peer * per_device + start + item for item in range(size))
        start += size
    delays = np.asarray(order)
    channel = np.arange(channels)
    angles = 2.0 * math.pi * (delays[:, None] * channel[None, :] % channels) / channels
    rows = np.stack([np.cos(angles), -np.sin(angles)], axis=1).reshape(channels, channels)
    return (rows * (window_taper(channels) / math.sqrt(channels))[None, :]).astype(np.float32)


def tap_table():
    distance = np.arange(HALF + 1, dtype=np.float32)
    table = np.zeros((HALF, HALF + 1), np.float32)
    for width in range(1, HALF + 1):
        spread = np.float32(width) * np.float32(0.5)
        profile = np.exp(-distance * distance / (np.float32(2.0) * spread * spread))
        profile = np.where(distance <= width, profile, np.float32(0.0)).astype(np.float32)
        total = profile[0] + np.float32(2.0) * np.sum(profile[1:], dtype=np.float32)
        table[width - 1] = profile / total
    return table


def band_table(out_places, in_places):
    taps = np.concatenate([tap_table(), np.zeros((HALF, 1), np.float32)], axis=1)
    distance = np.abs(np.asarray(out_places)[:, None] - np.asarray(in_places)[None, :])
    return taps[:, np.minimum(distance, HALF + 1)].astype(jnp.bfloat16)


def smooth_kernel(widths, mask, row_band, col_band, centre, top, bottom, left, right, corners, *outs):
    high, low, power, staged = outs
    block = centre.shape[0]
    outputs, columns = mask.shape
    first = pl.program_id(0) * block
    kept = mask[...]
    for group in range(0, block, PACK):
        members = range(group, group + PACK)
        chosen = pl.ds(group, PACK)
        flank = [left[chosen], right[chosen]]
        flank = jnp.concatenate([x.reshape(PACK * HALF, outputs) for x in flank], axis=0)
        corner = [corners[chosen, :HALF], corners[chosen, HALF:]]
        corner = jnp.concatenate([x.reshape(PACK * HALF, 2 * HALF) for x in corner], axis=0)
        flank = jnp.concatenate([flank, corner], axis=1).T
        half_smoothed = []
        for j in members:
            data = jnp.concatenate([centre[j], top[j], bottom[j]], axis=0)
            data = jnp.concatenate([data, flank], axis=1)
            band = row_band[widths[first + j] - 1]
            half_smoothed.append(
                jnp.dot(band, data, preferred_element_type=jnp.float32).astype(jnp.bfloat16)
            )
        for j, rows in zip(members, half_smoothed):
            band = col_band[(widths[first + j] - 1) * PACK + j % PACK]
            smoothed = jnp.dot(rows, band, preferred_element_type=jnp.float32)
            staged[pl.ds(j, outputs, stride=block), :] = smoothed * kept

    step = 8
    total = jnp.zeros((block, columns), jnp.float32)
    for start in range(0, outputs, step):
        value = staged[pl.ds(start * block, step * block), :]
        rounded = value.astype(jnp.bfloat16)
        rest = (value - rounded.astype(jnp.float32)).astype(jnp.bfloat16)
        high[pl.ds(start, step)] = rounded.reshape(step, block, columns)
        low[pl.ds(start, step)] = rest.reshape(step, block, columns)
        total = total + jnp.sum((value * value).reshape(step, block, columns), axis=0)
    power[...] = total


def smooth(half_widths, mask, pieces, row_band, col_band, block=32):
    centre = pieces[0]
    channels, _, columns = centre.shape
    outputs = mask.shape[0]
    whole = lambda shape: pl.BlockSpec(shape, lambda i: (0,) * len(shape))
    piece = lambda x: pl.BlockSpec((block,) + x.shape[1:], lambda i: (i, 0, 0))
    split_spec = pl.BlockSpec((outputs, block, columns), lambda i: (0, i, 0))
    split_shape = jax.ShapeDtypeStruct((outputs, channels, columns), jnp.bfloat16)
    tables = [mask, row_band, col_band]
    return pl.pallas_call(
        smooth_kernel,
        grid=(channels // block,),
        in_specs=[pl.BlockSpec(memory_space=pltpu.SMEM)]
        + [whole(t.shape) for t in tables]
        + [piece(x) for x in pieces],
        out_specs=[split_spec, split_spec, pl.BlockSpec((block, columns), lambda i: (i, 0))],
        out_shape=[
            split_shape,
            split_shape,
            jax.ShapeDtypeStruct((channels, columns), jnp.float32),
        ],
        scratch_shapes=[pltpu.VMEM((outputs * block, columns), jnp.float32)],
        compiler_params=pltpu.CompilerParams(vmem_limit_bytes=VMEM_LIMIT),
        cost_estimate=pl.CostEstimate(
            flops=4 * channels * outputs * columns * 256, bytes_accessed=80_000_000, transcendentals=0
        ),
        name="smooth",
    )(half_widths, *tables, *pieces)


def delay_kernel(modes, high, low, out, staged):
    rows = high.shape[0]
    count, _, columns = out.shape
    for pair in range(rows // 2):
        first, second = 2 * pair, 2 * pair + 1
        coarse = jnp.concatenate([high[first], high[second]], axis=1)
        fine = jnp.concatenate([low[first], low[second]], axis=1)
        both = jnp.dot(modes[...], coarse, preferred_element_type=jnp.float32)
        value = both[:count] + both[count:]
        value = value + jnp.dot(modes[:count], fine, preferred_element_type=jnp.float32)
        staged[pl.ds(first, count, stride=rows), :] = value[:, :columns]
        staged[pl.ds(second, count, stride=rows), :] = value[:, columns:]
    out[...] = staged[...].reshape(count, rows, columns).astype(jnp.bfloat16)


def delay_chunk(matrix, high, low, block=16):
    tile_rows, channels, columns = high.shape
    count = matrix.shape[0] // 2
    spec = pl.BlockSpec((block, channels, columns), lambda i: (i, 0, 0))
    return pl.pallas_call(
        delay_kernel,
        grid=(tile_rows // block,),
        in_specs=[pl.BlockSpec(matrix.shape, lambda i: (0, 0)), spec, spec],
        out_specs=pl.BlockSpec((count, block, columns), lambda i: (0, i, 0)),
        out_shape=jax.ShapeDtypeStruct((count, tile_rows, columns), jnp.bfloat16),
        scratch_shapes=[pltpu.VMEM((count * block, columns), jnp.float32)],
        compiler_params=pltpu.CompilerParams(vmem_limit_bytes=VMEM_LIMIT),
        cost_estimate=pl.CostEstimate(
            flops=6 * count * channels * tile_rows * columns,
            bytes_accessed=40_000_000,
            transcendentals=0,
        ),
        name="delays",
    )(matrix, high, low)


def spatial_kernel(row_count, col_count, has_previous, slab, col_table, row_table, *refs):
    out, halfway = refs[-2:]
    _, _, tile_rows, _ = slab.shape
    side = row_count * tile_rows
    for a in range(row_count):
        line = jnp.concatenate(
            [slab[a * col_count + b, k] for k in range(2) for b in range(col_count)], axis=1
        )
        part = jnp.dot(line, col_table[...], preferred_element_type=jnp.float32)
        part = part.astype(jnp.bfloat16)
        columns = part.shape[1] // 2
        halfway[pl.ds(a * tile_rows, tile_rows), :] = part[:, :columns]
        halfway[pl.ds(side + a * tile_rows, tile_rows), :] = part[:, columns:]
    step = side // 2
    for k in range(2):
        for s in range(side // step):
            rows = row_table[pl.ds(k * side + s * step, step), :]
            out[0, k, pl.ds(s * step, step), :] = jnp.dot(
                rows, halfway[...], preferred_element_type=jnp.float32
            )


def spatial_chunk(received, col_table, row_table, shape, start, previous):
    peers, parts, tile_rows, tile_cols = received.shape
    items = parts // 2
    side, columns = shape[2], shape[3]
    in_specs = [
        pl.BlockSpec((peers, 2, tile_rows, tile_cols), lambda i: (0, i, 0, 0)),
        pl.BlockSpec(col_table.shape, lambda i: (0, 0)),
        pl.BlockSpec(row_table.shape, lambda i: (0, 0)),
    ]
    operands = [received, col_table, row_table]
    aliases = {}
    if previous is not None:
        in_specs.append(pl.BlockSpec(memory_space=pl.ANY))
        operands.append(previous)
        aliases = {3: 0}
    return pl.pallas_call(
        functools.partial(
            spatial_kernel, side // tile_rows, columns // tile_cols, previous is not None
        ),
        grid=(items,),
        in_specs=in_specs,
        out_specs=pl.BlockSpec((1, 2, side, columns), lambda i: (start + i, 0, 0, 0)),
        out_shape=jax.ShapeDtypeStruct(shape, jnp.float32),
        scratch_shapes=[pltpu.VMEM((2 * side, columns), jnp.bfloat16)],
        input_output_aliases=aliases,
        compiler_params=pltpu.CompilerParams(vmem_limit_bytes=VMEM_LIMIT),
        cost_estimate=pl.CostEstimate(
            flops=16 * items * side * side * columns,
            bytes_accessed=items * 12 * side * columns,
            transcendentals=0,
        ),
        name="spatial",
    )(*operands)


def shifted(x, axis, step):
    size = lax.axis_size(axis)
    pairs = [(i, i + step) for i in range(size) if 0 <= i + step < size]
    order = Layout(major_to_minor=tuple(range(x.ndim)))
    x = with_layout_constraint(x, order)
    return with_layout_constraint(lax.ppermute(x, axis, pairs), order)


def split_high_low(x):
    rounded = lax.reduce_precision(x, exponent_bits=8, mantissa_bits=7)
    return rounded.astype(jnp.bfloat16), (x - rounded).astype(jnp.bfloat16)


def chunk_sizes(per_device):
    if per_device <= 4 * END_DELAYS:
        return [per_device]
    return [END_DELAYS, per_device - 2 * END_DELAYS, END_DELAYS]


def tiled_body(sky_cube, half_widths, pixel_mask, foreground_modes):
    tile_rows, tile_cols, channels = sky_cube.shape
    row_count, col_count = lax.axis_size("row"), lax.axis_size("col")
    peers = row_count * col_count
    per_device = channels // 2 // peers
    sides, columns = row_count * tile_rows, col_count * tile_cols

    top = shifted(sky_cube[LAST], "row", 1)
    bottom = shifted(sky_cube[FIRST], "row", -1)
    left = shifted(sky_cube[:, LAST], "col", 1)
    right = shifted(sky_cube[:, FIRST], "col", -1)
    centre = jnp.transpose(sky_cube, (2, 0, 1))
    left, right, centre = lax.optimization_barrier((left, right, centre))
    ends = [jnp.concatenate([left[rows], right[rows]], axis=1) for rows in (LAST, FIRST)]
    corner = jnp.concatenate([shifted(ends[0], "row", 1), shifted(ends[1], "row", -1)], axis=0)
    pieces = [centre] + [jnp.transpose(x, (2, 0, 1)) for x in (top, bottom)]
    pieces += [jnp.transpose(x, (2, 1, 0)) for x in (left, right, corner)]

    def places(length):
        return list(range(length)) + list(range(-HALF, 0)) + list(range(length, length + HALF))

    row_band = band_table(list(range(tile_rows)), places(tile_rows))
    narrow = np.swapaxes(band_table(list(range(tile_cols)), places(tile_cols)), 1, 2)
    col_band = np.zeros((HALF, PACK, tile_cols + PACK * 2 * HALF, tile_cols), narrow.dtype)
    col_band[:, :, :tile_cols] = narrow[:, None, :tile_cols]
    for member in range(PACK):
        for part in range(2):
            to = tile_cols + (part * PACK + member) * HALF
            begin = tile_cols + part * HALF
            col_band[:, member, to : to + HALF] = narrow[:, begin : begin + HALF]
    col_band = col_band.reshape((HALF * PACK,) + col_band.shape[2:])
    high, low, power = smooth(
        half_widths, pixel_mask.astype(jnp.float32), pieces, row_band, col_band
    )

    sizes = chunk_sizes(per_device)
    delay_table = delay_rows(channels, peers, sizes)
    mode_delays = jnp.dot(
        delay_table, foreground_modes.T, precision=highest, preferred_element_type=jnp.float32
    )
    tile_power = jnp.broadcast_to(jnp.sum(power, axis=1)[None], (peers, channels))
    power_sum = jnp.sum(
        lax.all_to_all(tile_power, ("row", "col"), split_axis=0, concat_axis=0, tiled=True), axis=0
    )
    weights = 1.0 / (power_sum / (sides * columns) + 1e-05)
    channel_weights = weights / jnp.mean(weights)
    weighted_modes = foreground_modes * weights[None, :]
    normal_matrix = jnp.dot(
        weighted_modes, foreground_modes.T, precision=highest, preferred_element_type=jnp.float32
    )
    factor = jnp.linalg.cholesky(normal_matrix)
    solved = jax.scipy.linalg.cho_solve((factor, True), weighted_modes)
    matrix = delay_table - jnp.dot(
        mode_delays, solved, precision=highest, preferred_element_type=jnp.float32
    )
    matrix_high, matrix_low = split_high_low(matrix)

    cos_c, sin_c = dft_parts(columns)
    col_table = np.block([[cos_c, sin_c], [-sin_c, cos_c]])
    cos_r, sin_r = dft_parts(sides)
    row_table = np.block([[cos_r, -sin_r], [sin_r, cos_r]])

    spectrum = None
    start = 0
    for index, size in enumerate(sizes):
        begin, count = 2 * start * peers, 2 * size * peers
        both = jnp.concatenate(
            [matrix_high[begin : begin + count], matrix_low[begin : begin + count]], axis=0
        )
        delays = delay_chunk(both, high, low)
        delays = delays.reshape(peers, 2 * size, tile_rows, tile_cols)
        if index == 2:
            delays, spectrum = lax.optimization_barrier((delays, spectrum))
        received = lax.all_to_all(delays, ("row", "col"), split_axis=0, concat_axis=0, tiled=True)
        if index == 1:
            held = received
            spectrum = spatial_chunk(
                first_received, col_table, row_table, (per_device, 2, sides, columns), 0, None
            )
        elif index == 2:
            spectrum = spatial_chunk(
                held, col_table, row_table, spectrum.shape, sizes[0], spectrum
            )
            spectrum = spatial_chunk(received, col_table, row_table, spectrum.shape, start, spectrum)
        else:
            first_received = received
        start += size
    if len(sizes) == 1:
        spectrum = spatial_chunk(
            first_received, col_table, row_table, (per_device, 2, sides, columns), 0, None
        )
    return (spectrum, channel_weights)


def small_tile_body(sky_cube, half_widths, pixel_mask, foreground_modes):
    tile_rows, tile_cols, channels = sky_cube.shape
    row_count, col_count = lax.axis_size("row"), lax.axis_size("col")
    peers = row_count * col_count
    per_device = channels // 2 // peers
    sides, columns = row_count * tile_rows, col_count * tile_cols
    beam_taps = make_taps(half_widths)
    extended = padded(sky_cube, (("row", 0),), HALF)
    row_part = jnp.einsum(
        "oif,icf->ocf",
        banded_taps(tile_rows, beam_taps),
        extended,
        preferred_element_type=jnp.float32,
    ).astype(jnp.bfloat16)
    row_smoothed = padded(row_part, (("col", 1),), HALF)
    smoothed = jnp.einsum(
        "oif,rif->rof",
        banded_taps(tile_cols, beam_taps),
        row_smoothed,
        preferred_element_type=jnp.float32,
    )
    masked = pixel_mask.astype(jnp.float32)[:, :, None] * smoothed
    pixels = masked.reshape(tile_rows * tile_cols, channels)
    power_sum = lax.psum(jnp.sum(masked * masked, axis=(0, 1)), ("row", "col"))
    weights = 1.0 / (power_sum / (sides * columns) + 1e-05)
    channel_weights = weights / jnp.mean(weights)
    weighted_modes = foreground_modes * weights[None, :]
    normal_matrix = jnp.dot(
        weighted_modes, foreground_modes.T, precision=highest, preferred_element_type=jnp.float32
    )
    projected = jnp.dot(
        pixels, weighted_modes.T, precision=highest, preferred_element_type=jnp.float32
    )
    factor = jnp.linalg.cholesky(normal_matrix)
    amplitude = jax.scipy.linalg.cho_solve((factor, True), projected.T)
    cleaned = pixels - jnp.dot(
        amplitude.T, foreground_modes, precision=highest, preferred_element_type=jnp.float32
    )
    delay_tile = lax.dot_general(
        delay_rows(channels, peers, [per_device]),
        cleaned,
        (((1,), (1,)), ((), ())),
        precision=highest,
        preferred_element_type=jnp.float32,
    )
    sendable = delay_tile.astype(jnp.bfloat16).reshape(
        peers, per_device, 2, tile_rows, tile_cols
    )
    regrouped = lax.all_to_all(sendable, ("row", "col"), split_axis=0, concat_axis=0, tiled=True)
    slab = regrouped.reshape(row_count, col_count, per_device, 2, tile_rows, tile_cols)
    slab = slab.transpose(2, 3, 0, 4, 1, 5).reshape(per_device, 2, sides, columns)
    cos_c, sin_c = dft_parts(columns)
    col_table = np.stack([np.stack([cos_c, -sin_c]), np.stack([sin_c, cos_c])])
    cos_r, sin_r = dft_parts(sides)
    row_table = np.stack([np.stack([cos_r, -sin_r]), np.stack([sin_r, cos_r])])
    halfway = jnp.einsum(
        "kmrc,nmcd->knrd", slab, col_table, preferred_element_type=jnp.float32
    ).astype(jnp.bfloat16)
    spectrum = jnp.einsum(
        "nmsr,kmrd->knsd", row_table, halfway, preferred_element_type=jnp.float32
    )
    return (spectrum, channel_weights)


def body(sky_cube, half_widths, pixel_mask, foreground_modes):
    tile_rows, tile_cols, channels = sky_cube.shape
    fits = tile_rows % 128 == 0 and tile_cols % 128 == 0 and channels % 128 == 0
    run = tiled_body if fits else small_tile_body
    return run(sky_cube, half_widths, pixel_mask, foreground_modes)


def solution(mesh):
    return jax.shard_map(
        body,
        mesh=mesh,
        in_specs=(P(("grp", "row"), "col", None), P(), P(("grp", "row"), "col"), P("grp", None)),
        out_specs=(P(("grp", "row", "col"), None, None, None), P("grp")),
        check_vma=False,
    )
```

```python
import functools
import math

import jax
import jax.numpy as jnp
import numpy as np
from jax import lax
from jax.experimental import pallas as pl
from jax.experimental.layout import Layout, with_layout_constraint
from jax.experimental.pallas import tpu as pltpu
from jax.sharding import PartitionSpec as P

HALF = 16
VMEM_LIMIT = 48 * 1024 * 1024
PACK = 4
TURN = 8
HEAD_ROWS = 16
FIRST, LAST = slice(0, HALF), slice(-HALF, None)
END_DELAYS = 2

highest = lax.Precision.HIGHEST


def padded(x, sides, width):
    for axis, dim in sides:
        size, length = (lax.axis_size(axis), x.shape[dim])
        up = [(i, (i + 1) % size) for i in range(size - 1)]
        down = [(j, i) for i, j in up]
        last = lax.slice_in_dim(x, length - width, length, axis=dim)
        initial = lax.slice_in_dim(x, 0, width, axis=dim)
        before = lax.ppermute(last, axis, up)
        after = lax.ppermute(initial, axis, down)
        x = jnp.concatenate([before, x, after], axis=dim)
    return x


def make_taps(half_widths):
    offsets = jnp.arange(2 * HALF + 1, dtype=jnp.int32) - HALF
    distance = offsets.astype(jnp.float32)[:, None]
    spread = half_widths.astype(jnp.float32)[None, :] * 0.5
    inside = jnp.abs(offsets)[:, None] <= half_widths[None, :]
    profile = jnp.where(
        inside, jnp.exp(-distance * distance / (2.0 * spread * spread)), jnp.float32(0.0)
    )
    return (profile / jnp.sum(profile, axis=0, keepdims=True)).astype(jnp.bfloat16)


def banded_taps(outputs, beam_taps):
    offsets = (
        jnp.arange(outputs + 2 * HALF, dtype=jnp.int32)[None, :]
        - jnp.arange(outputs, dtype=jnp.int32)[:, None]
    )
    one_hot = (
        offsets[:, :, None] == jnp.arange(2 * HALF + 1, dtype=jnp.int32)[None, None, :]
    ).astype(jnp.bfloat16)
    return jnp.einsum("oit,tf->oif", one_hot, beam_taps, preferred_element_type=jnp.float32).astype(
        jnp.bfloat16
    )


def window_taper(length):
    angles = 2.0 * math.pi * np.arange(length) / (length - 1)
    return (
        0.35875
        - 0.48829 * np.cos(angles)
        + 0.14128 * np.cos(2.0 * angles)
        - 0.01168 * np.cos(3.0 * angles)
    )


def dft_parts(length):
    indices = np.arange(length)
    angles = 2.0 * math.pi * (indices[:, None] * indices[None, :] % length) / length
    scale = 1.0 / math.sqrt(length)
    return (
        (np.cos(angles) * scale).astype(jnp.bfloat16),
        (-np.sin(angles) * scale).astype(jnp.bfloat16),
    )


def delay_rows(channels, peers, sizes):
    per_device = channels // 2 // peers
    order, start = [], 0
    for size in sizes:
        for peer in range(peers):
            order.extend(peer * per_device + start + item for item in range(size))
        start += size
    delays = np.asarray(order)
    channel = np.arange(channels)
    angles = 2.0 * math.pi * (delays[:, None] * channel[None, :] % channels) / channels
    rows = np.stack([np.cos(angles), -np.sin(angles)], axis=1).reshape(channels, channels)
    return (rows * (window_taper(channels) / math.sqrt(channels))[None, :]).astype(np.float32)


def tap_table():
    distance = np.arange(HALF + 1, dtype=np.float32)
    table = np.zeros((HALF, HALF + 1), np.float32)
    for width in range(1, HALF + 1):
        spread = np.float32(width) * np.float32(0.5)
        profile = np.exp(-distance * distance / (np.float32(2.0) * spread * spread))
        profile = np.where(distance <= width, profile, np.float32(0.0)).astype(np.float32)
        total = profile[0] + np.float32(2.0) * np.sum(profile[1:], dtype=np.float32)
        table[width - 1] = profile / total
    return table


def band_table(out_places, in_places):
    taps = np.concatenate([tap_table(), np.zeros((HALF, 1), np.float32)], axis=1)
    distance = np.abs(np.asarray(out_places)[:, None] - np.asarray(in_places)[None, :])
    return taps[:, np.minimum(distance, HALF + 1)].astype(jnp.bfloat16)


def smooth_kernel(widths, mask, row_band, col_band, centre, top, bottom, left, right, *outs):
    high, low, power, staged = outs
    block = centre.shape[0]
    outputs, columns = mask.shape
    first = pl.program_id(0) * block
    kept = mask[...]
    done = []
    for group in range(0, block, PACK):
        members = range(group, group + PACK)
        chosen = pl.ds(group, PACK)
        flank = jnp.concatenate([left[chosen], right[chosen]], axis=1)
        flank = flank.reshape(PACK * 2 * HALF, outputs).T
        caps = [jnp.concatenate([top[j], bottom[j]], axis=0) for j in members]
        corner = jnp.concatenate([x[:, columns:] for x in caps], axis=1)
        flank = jnp.concatenate([flank, corner], axis=0)
        half_smoothed = []
        for j, cap in zip(members, caps):
            data = jnp.concatenate([centre[j], cap[:, :columns]], axis=0)
            data = jnp.concatenate([data, flank], axis=1)
            band = row_band[widths[first + j] - 1]
            half_smoothed.append(
                jnp.dot(band, data, preferred_element_type=jnp.float32).astype(jnp.bfloat16)
            )
        for j, rows in zip(members, half_smoothed):
            band = col_band[(widths[first + j] - 1) * PACK + j % PACK]
            smoothed = jnp.dot(rows, band, preferred_element_type=jnp.float32)
            done.append(smoothed * kept)
        if len(done) == TURN:
            begin = group + PACK - TURN
            staged[:, pl.ds(begin, TURN), :] = jnp.swapaxes(jnp.stack(done), 0, 1)
            done = []

    step = 8
    total = jnp.zeros((block, columns), jnp.float32)
    for start in range(0, outputs, step):
        value = staged[pl.ds(start, step)]
        rounded = value.astype(jnp.bfloat16)
        high[pl.ds(start, step)] = rounded
        low[pl.ds(start, step)] = (value - rounded.astype(jnp.float32)).astype(jnp.bfloat16)
        total = total + jnp.sum(value * value, axis=0)
    power[...] = total


def smooth(half_widths, mask, pieces, row_band, col_band, block=32):
    centre = pieces[0]
    channels, _, columns = centre.shape
    outputs = mask.shape[0]
    whole = lambda shape: pl.BlockSpec(shape, lambda i: (0,) * len(shape))
    piece = lambda x: pl.BlockSpec((block,) + x.shape[1:], lambda i: (i, 0, 0))
    split_spec = pl.BlockSpec((outputs, block, columns), lambda i: (0, i, 0))
    split_shape = jax.ShapeDtypeStruct((outputs, channels, columns), jnp.bfloat16)
    tables = [mask, row_band, col_band]
    return pl.pallas_call(
        smooth_kernel,
        grid=(channels // block,),
        in_specs=[pl.BlockSpec(memory_space=pltpu.SMEM)]
        + [whole(t.shape) for t in tables]
        + [piece(x) for x in pieces],
        out_specs=[split_spec, split_spec, pl.BlockSpec((block, columns), lambda i: (i, 0))],
        out_shape=[
            split_shape,
            split_shape,
            jax.ShapeDtypeStruct((channels, columns), jnp.float32),
        ],
        scratch_shapes=[pltpu.VMEM((outputs, block, columns), jnp.float32)],
        compiler_params=pltpu.CompilerParams(vmem_limit_bytes=VMEM_LIMIT),
        cost_estimate=pl.CostEstimate(
            flops=4 * channels * outputs * columns * 256, bytes_accessed=80_000_000, transcendentals=0
        ),
        name="smooth",
    )(half_widths, *tables, *pieces)


def delay_kernel(modes, high, low, out, staged):
    rows = high.shape[0]
    count, _, columns = out.shape
    for pair in range(rows // 2):
        first, second = 2 * pair, 2 * pair + 1
        coarse = jnp.concatenate([high[first], high[second]], axis=1)
        fine = jnp.concatenate([low[first], low[second]], axis=1)
        both = jnp.dot(modes[...], coarse, preferred_element_type=jnp.float32)
        value = both[:count] + both[count:]
        value = value + jnp.dot(modes[:count], fine, preferred_element_type=jnp.float32)
        staged[pl.ds(first, count, stride=rows), :] = value[:, :columns]
        staged[pl.ds(second, count, stride=rows), :] = value[:, columns:]
    out[...] = staged[...].reshape(count, rows, columns).astype(jnp.bfloat16)


def delay_chunk(matrix, high, low, begin, rows, block=16):
    _, channels, columns = high.shape
    count = matrix.shape[0] // 2
    spec = pl.BlockSpec((block, channels, columns), lambda i: (begin // block + i, 0, 0))
    return pl.pallas_call(
        delay_kernel,
        grid=(rows // block,),
        in_specs=[pl.BlockSpec(matrix.shape, lambda i: (0, 0)), spec, spec],
        out_specs=pl.BlockSpec((count, block, columns), lambda i: (0, i, 0)),
        out_shape=jax.ShapeDtypeStruct((count, rows, columns), jnp.bfloat16),
        scratch_shapes=[pltpu.VMEM((count * block, columns), jnp.float32)],
        compiler_params=pltpu.CompilerParams(vmem_limit_bytes=VMEM_LIMIT),
        cost_estimate=pl.CostEstimate(
            flops=6 * count * channels * rows * columns,
            bytes_accessed=(4 * channels + 2 * count) * rows * columns,
            transcendentals=0,
        ),
        name="delays",
    )(matrix, high, low)


def spatial_kernel(row_count, col_count, head, tail, col_table, row_table, *refs):
    out, halfway = refs[-2:]
    tile_rows = head.shape[2] + tail.shape[2]
    side = row_count * tile_rows
    for a in range(row_count):
        line = jnp.concatenate(
            [
                jnp.concatenate(
                    [slab[a * col_count + b, k] for k in range(2) for b in range(col_count)], axis=1
                )
                for slab in (head, tail)
            ],
            axis=0,
        )
        part = jnp.dot(line, col_table[...], preferred_element_type=jnp.float32)
        part = part.astype(jnp.bfloat16)
        columns = part.shape[1] // 2
        halfway[pl.ds(a * tile_rows, tile_rows), :] = part[:, :columns]
        halfway[pl.ds(side + a * tile_rows, tile_rows), :] = part[:, columns:]
    step = side // 2
    for k in range(2):
        for s in range(side // step):
            rows = row_table[pl.ds(k * side + s * step, step), :]
            out[0, k, pl.ds(s * step, step), :] = jnp.dot(
                rows, halfway[...], preferred_element_type=jnp.float32
            )


def spatial_chunk(head, tail, col_table, row_table, shape, start, previous):
    peers, parts, tail_rows, tile_cols = tail.shape
    items, head_rows = parts // 2, head.shape[2]
    side, columns = shape[2], shape[3]
    row_count, col_count = side // (head_rows + tail_rows), columns // tile_cols
    in_specs = [
        pl.BlockSpec((peers, 2, head_rows, tile_cols), lambda i: (0, start + i, 0, 0)),
        pl.BlockSpec((peers, 2, tail_rows, tile_cols), lambda i: (0, i, 0, 0)),
        pl.BlockSpec(col_table.shape, lambda i: (0, 0)),
        pl.BlockSpec(row_table.shape, lambda i: (0, 0)),
    ]
    operands = [head, tail, col_table, row_table]
    aliases = {}
    if previous is not None:
        in_specs.append(pl.BlockSpec(memory_space=pl.ANY))
        operands.append(previous)
        aliases = {4: 0}
    return pl.pallas_call(
        functools.partial(spatial_kernel, row_count, col_count),
        grid=(items,),
        in_specs=in_specs,
        out_specs=pl.BlockSpec((1, 2, side, columns), lambda i: (start + i, 0, 0, 0)),
        out_shape=jax.ShapeDtypeStruct(shape, jnp.float32),
        scratch_shapes=[pltpu.VMEM((2 * side, columns), jnp.bfloat16)],
        input_output_aliases=aliases,
        compiler_params=pltpu.CompilerParams(vmem_limit_bytes=VMEM_LIMIT),
        cost_estimate=pl.CostEstimate(
            flops=16 * items * side * side * columns,
            bytes_accessed=items * 12 * side * columns,
            transcendentals=0,
        ),
        name="spatial",
    )(*operands)


def pinned(x):
    return with_layout_constraint(x, Layout(major_to_minor=tuple(range(x.ndim))))


def shifted(x, axis, step):
    size = lax.axis_size(axis)
    pairs = [(i, i + step) for i in range(size) if 0 <= i + step < size]
    return pinned(lax.ppermute(pinned(x), axis, pairs))


def split_high_low(x):
    rounded = lax.reduce_precision(x, exponent_bits=8, mantissa_bits=7)
    return rounded.astype(jnp.bfloat16), (x - rounded).astype(jnp.bfloat16)


def chunk_sizes(per_device):
    if per_device <= 4 * END_DELAYS:
        return [per_device]
    return [per_device - END_DELAYS, END_DELAYS]


def tiled_body(sky_cube, half_widths, pixel_mask, foreground_modes):
    tile_rows, tile_cols, channels = sky_cube.shape
    row_count, col_count = lax.axis_size("row"), lax.axis_size("col")
    peers = row_count * col_count
    per_device = channels // 2 // peers
    sides, columns = row_count * tile_rows, col_count * tile_cols

    sky_cube, last, initial = lax.optimization_barrier((sky_cube, sky_cube[LAST], sky_cube[FIRST]))
    top, bottom = shifted(last, "row", 1), shifted(initial, "row", -1)
    left, right = shifted(sky_cube[:, LAST], "col", 1), shifted(sky_cube[:, FIRST], "col", -1)
    centre = jnp.transpose(sky_cube, (2, 0, 1))
    left, right, centre = lax.optimization_barrier((left, right, centre))
    ends = [jnp.concatenate([left[rows], right[rows]], axis=1) for rows in (LAST, FIRST)]
    corners = [shifted(ends[0], "row", 1), shifted(ends[1], "row", -1)]
    caps = [pinned(jnp.concatenate([x, y], axis=1)) for x, y in zip((top, bottom), corners)]
    pieces = [centre] + [jnp.transpose(x, (2, 0, 1)) for x in caps]
    pieces += [jnp.transpose(x, (2, 1, 0)) for x in (left, right)]

    def places(length):
        return list(range(length)) + list(range(-HALF, 0)) + list(range(length, length + HALF))

    row_band = band_table(list(range(tile_rows)), places(tile_rows))
    narrow = np.swapaxes(band_table(list(range(tile_cols)), places(tile_cols)), 1, 2)
    col_band = np.zeros((HALF, PACK, tile_cols + PACK * 2 * HALF, tile_cols), narrow.dtype)
    col_band[:, :, :tile_cols] = narrow[:, None, :tile_cols]
    for member in range(PACK):
        begin = tile_cols + member * 2 * HALF
        col_band[:, member, begin : begin + 2 * HALF] = narrow[:, tile_cols:]
    col_band = col_band.reshape((HALF * PACK,) + col_band.shape[2:])
    high, low, power = smooth(
        half_widths, pixel_mask.astype(jnp.float32), pieces, row_band, col_band
    )

    delay_table = delay_rows(channels, peers, [per_device])
    mode_delays = jnp.dot(
        delay_table, foreground_modes.T, precision=highest, preferred_element_type=jnp.float32
    )
    tile_power = jnp.broadcast_to(jnp.sum(power, axis=1)[None], (peers, channels))
    power_sum = jnp.sum(
        lax.all_to_all(tile_power, ("row", "col"), split_axis=0, concat_axis=0, tiled=True), axis=0
    )
    weights = 1.0 / (power_sum / (sides * columns) + 1e-05)
    channel_weights = weights / jnp.mean(weights)
    weighted_modes = foreground_modes * weights[None, :]
    normal_matrix = jnp.dot(
        weighted_modes, foreground_modes.T, precision=highest, preferred_element_type=jnp.float32
    )
    factor = jnp.linalg.cholesky(normal_matrix)
    solved = jax.scipy.linalg.cho_solve((factor, True), weighted_modes)
    matrix = delay_table - jnp.dot(
        mode_delays, solved, precision=highest, preferred_element_type=jnp.float32
    )
    matrix_high, matrix_low = split_high_low(matrix)

    cos_c, sin_c = dft_parts(columns)
    col_table = np.block([[cos_c, sin_c], [-sin_c, cos_c]])
    cos_r, sin_r = dft_parts(sides)
    row_table = np.block([[cos_r, -sin_r], [sin_r, cos_r]])

    def send(begin, end, first_row, rows):
        parts = [
            x.reshape(peers, per_device, 2, channels)[:, begin:end].reshape(-1, channels)
            for x in (matrix_high, matrix_low)
        ]
        delays = delay_chunk(jnp.concatenate(parts, axis=0), high, low, first_row, rows)
        return delays.reshape(peers, 2 * (end - begin), rows, tile_cols)

    def exchange(x):
        return lax.all_to_all(x, ("row", "col"), split_axis=0, concat_axis=0, tiled=True)

    shape = (per_device, 2, sides, columns)
    head = exchange(send(0, per_device, 0, HEAD_ROWS))
    tail_rows = tile_rows - HEAD_ROWS
    spectrum = None
    start = 0
    for size in chunk_sizes(per_device):
        tail = exchange(send(start, start + size, HEAD_ROWS, tail_rows))
        spectrum = spatial_chunk(head, tail, col_table, row_table, shape, start, spectrum)
        start += size
    return (spectrum, channel_weights)


def small_tile_body(sky_cube, half_widths, pixel_mask, foreground_modes):
    tile_rows, tile_cols, channels = sky_cube.shape
    row_count, col_count = lax.axis_size("row"), lax.axis_size("col")
    peers = row_count * col_count
    per_device = channels // 2 // peers
    sides, columns = row_count * tile_rows, col_count * tile_cols
    beam_taps = make_taps(half_widths)
    extended = padded(sky_cube, (("row", 0),), HALF)
    row_part = jnp.einsum(
        "oif,icf->ocf",
        banded_taps(tile_rows, beam_taps),
        extended,
        preferred_element_type=jnp.float32,
    ).astype(jnp.bfloat16)
    row_smoothed = padded(row_part, (("col", 1),), HALF)
    smoothed = jnp.einsum(
        "oif,rif->rof",
        banded_taps(tile_cols, beam_taps),
        row_smoothed,
        preferred_element_type=jnp.float32,
    )
    masked = pixel_mask.astype(jnp.float32)[:, :, None] * smoothed
    pixels = masked.reshape(tile_rows * tile_cols, channels)
    power_sum = lax.psum(jnp.sum(masked * masked, axis=(0, 1)), ("row", "col"))
    weights = 1.0 / (power_sum / (sides * columns) + 1e-05)
    channel_weights = weights / jnp.mean(weights)
    weighted_modes = foreground_modes * weights[None, :]
    normal_matrix = jnp.dot(
        weighted_modes, foreground_modes.T, precision=highest, preferred_element_type=jnp.float32
    )
    projected = jnp.dot(
        pixels, weighted_modes.T, precision=highest, preferred_element_type=jnp.float32
    )
    factor = jnp.linalg.cholesky(normal_matrix)
    amplitude = jax.scipy.linalg.cho_solve((factor, True), projected.T)
    cleaned = pixels - jnp.dot(
        amplitude.T, foreground_modes, precision=highest, preferred_element_type=jnp.float32
    )
    delay_tile = lax.dot_general(
        delay_rows(channels, peers, [per_device]),
        cleaned,
        (((1,), (1,)), ((), ())),
        precision=highest,
        preferred_element_type=jnp.float32,
    )
    sendable = delay_tile.astype(jnp.bfloat16).reshape(
        peers, per_device, 2, tile_rows, tile_cols
    )
    regrouped = lax.all_to_all(sendable, ("row", "col"), split_axis=0, concat_axis=0, tiled=True)
    slab = regrouped.reshape(row_count, col_count, per_device, 2, tile_rows, tile_cols)
    slab = slab.transpose(2, 3, 0, 4, 1, 5).reshape(per_device, 2, sides, columns)
    cos_c, sin_c = dft_parts(columns)
    col_table = np.stack([np.stack([cos_c, -sin_c]), np.stack([sin_c, cos_c])])
    cos_r, sin_r = dft_parts(sides)
    row_table = np.stack([np.stack([cos_r, -sin_r]), np.stack([sin_r, cos_r])])
    halfway = jnp.einsum(
        "kmrc,nmcd->knrd", slab, col_table, preferred_element_type=jnp.float32
    ).astype(jnp.bfloat16)
    spectrum = jnp.einsum(
        "nmsr,kmrd->knsd", row_table, halfway, preferred_element_type=jnp.float32
    )
    return (spectrum, channel_weights)


def body(sky_cube, half_widths, pixel_mask, foreground_modes):
    tile_rows, tile_cols, channels = sky_cube.shape
    fits = tile_rows % 128 == 0 and tile_cols % 128 == 0 and channels % 128 == 0
    run = tiled_body if fits else small_tile_body
    return run(sky_cube, half_widths, pixel_mask, foreground_modes)


def solution(mesh):
    return jax.shard_map(
        body,
        mesh=mesh,
        in_specs=(P(("grp", "row"), "col", None), P(), P(("grp", "row"), "col"), P("grp", None)),
        out_specs=(P(("grp", "row", "col"), None, None, None), P("grp")),
        check_vma=False,
    )
```

```python
import functools
import math

import jax
import jax.numpy as jnp
import numpy as np
from jax import lax
from jax.experimental import pallas as pl
from jax.experimental.layout import Layout, with_layout_constraint
from jax.experimental.pallas import tpu as pltpu
from jax.sharding import PartitionSpec as P

HALF = 16
VMEM_LIMIT = 48 * 1024 * 1024
PACK = 4
TURN = 8
HEAD_ROWS = 48
LANES = 128
FIRST, LAST = slice(0, HALF), slice(-HALF, None)
END_DELAYS = 2

highest = lax.Precision.HIGHEST


def padded(x, sides, width):
    for axis, dim in sides:
        size, length = (lax.axis_size(axis), x.shape[dim])
        up = [(i, (i + 1) % size) for i in range(size - 1)]
        down = [(j, i) for i, j in up]
        last = lax.slice_in_dim(x, length - width, length, axis=dim)
        initial = lax.slice_in_dim(x, 0, width, axis=dim)
        before = lax.ppermute(last, axis, up)
        after = lax.ppermute(initial, axis, down)
        x = jnp.concatenate([before, x, after], axis=dim)
    return x


def make_taps(half_widths):
    offsets = jnp.arange(2 * HALF + 1, dtype=jnp.int32) - HALF
    distance = offsets.astype(jnp.float32)[:, None]
    spread = half_widths.astype(jnp.float32)[None, :] * 0.5
    inside = jnp.abs(offsets)[:, None] <= half_widths[None, :]
    profile = jnp.where(
        inside, jnp.exp(-distance * distance / (2.0 * spread * spread)), jnp.float32(0.0)
    )
    return (profile / jnp.sum(profile, axis=0, keepdims=True)).astype(jnp.bfloat16)


def banded_taps(outputs, beam_taps):
    offsets = (
        jnp.arange(outputs + 2 * HALF, dtype=jnp.int32)[None, :]
        - jnp.arange(outputs, dtype=jnp.int32)[:, None]
    )
    one_hot = (
        offsets[:, :, None] == jnp.arange(2 * HALF + 1, dtype=jnp.int32)[None, None, :]
    ).astype(jnp.bfloat16)
    return jnp.einsum("oit,tf->oif", one_hot, beam_taps, preferred_element_type=jnp.float32).astype(
        jnp.bfloat16
    )


def window_taper(length):
    angles = 2.0 * math.pi * np.arange(length) / (length - 1)
    return (
        0.35875
        - 0.48829 * np.cos(angles)
        + 0.14128 * np.cos(2.0 * angles)
        - 0.01168 * np.cos(3.0 * angles)
    )


def dft_parts(length):
    indices = np.arange(length)
    angles = 2.0 * math.pi * (indices[:, None] * indices[None, :] % length) / length
    scale = 1.0 / math.sqrt(length)
    return (
        (np.cos(angles) * scale).astype(jnp.bfloat16),
        (-np.sin(angles) * scale).astype(jnp.bfloat16),
    )


def delay_rows(channels, peers, sizes):
    per_device = channels // 2 // peers
    order, start = [], 0
    for size in sizes:
        for peer in range(peers):
            order.extend(peer * per_device + start + item for item in range(size))
        start += size
    delays = np.asarray(order)
    channel = np.arange(channels)
    angles = 2.0 * math.pi * (delays[:, None] * channel[None, :] % channels) / channels
    rows = np.stack([np.cos(angles), -np.sin(angles)], axis=1).reshape(channels, channels)
    return (rows * (window_taper(channels) / math.sqrt(channels))[None, :]).astype(np.float32)


def tap_table():
    distance = np.arange(HALF + 1, dtype=np.float32)
    table = np.zeros((HALF, HALF + 1), np.float32)
    for width in range(1, HALF + 1):
        spread = np.float32(width) * np.float32(0.5)
        profile = np.exp(-distance * distance / (np.float32(2.0) * spread * spread))
        profile = np.where(distance <= width, profile, np.float32(0.0)).astype(np.float32)
        total = profile[0] + np.float32(2.0) * np.sum(profile[1:], dtype=np.float32)
        table[width - 1] = profile / total
    return table


def band_table(out_places, in_places):
    taps = np.concatenate([tap_table(), np.zeros((HALF, 1), np.float32)], axis=1)
    distance = np.abs(np.asarray(out_places)[:, None] - np.asarray(in_places)[None, :])
    return taps[:, np.minimum(distance, HALF + 1)].astype(jnp.bfloat16)


def smooth_kernel(spans, capped, widths, mask, row_band, col_band, centre, left, right, *refs):
    if capped:
        top, bottom, top_ends, bottom_ends, *refs = refs
        high, low, power, staged, sides, caps, corners = refs
    else:
        high, low, power, staged, sides = refs
    block = centre.shape[0]
    outputs, columns = mask.shape
    rows = sides.shape[2]
    step = pl.program_id(0)
    per_turn = LANES // block

    @pl.when(step % per_turn == 0)
    def _():
        sides[:, FIRST] = jnp.transpose(left[...], (2, 1, 0))
        sides[:, HALF : 2 * HALF] = jnp.transpose(right[...], (2, 1, 0))
        if capped:
            caps[:, FIRST] = jnp.transpose(top[...], (2, 0, 1))
            caps[:, HALF : 2 * HALF] = jnp.transpose(bottom[...], (2, 0, 1))
            corners[:, FIRST] = jnp.transpose(top_ends[...], (2, 0, 1))
            corners[:, HALF : 2 * HALF] = jnp.transpose(bottom_ends[...], (2, 0, 1))

    first = step * block
    lane = (step % per_turn) * block
    kept = mask[...]
    done = []
    for group in range(0, block, PACK):
        members = range(group, group + PACK)
        flank = sides[pl.ds(lane + group, PACK)].reshape(PACK * 2 * HALF, rows).T
        flank = [flank[a:b] for a, b in spans]
        if capped:
            corner = [corners[lane + j] for j in members]
            flank.append(jnp.concatenate(corner, axis=1))
        flank = jnp.concatenate(flank, axis=0)
        half_smoothed = []
        for j in members:
            data = [centre[j, a:b] for a, b in spans]
            if capped:
                data.append(caps[lane + j])
            data = jnp.concatenate([jnp.concatenate(data, axis=0), flank], axis=1)
            band = row_band[widths[first + j] - 1]
            half_smoothed.append(
                jnp.dot(band, data, preferred_element_type=jnp.float32).astype(jnp.bfloat16)
            )
        for j, half in zip(members, half_smoothed):
            band = col_band[(widths[first + j] - 1) * PACK + j % PACK]
            smoothed = jnp.dot(half, band, preferred_element_type=jnp.float32)
            done.append(smoothed * kept)
        if len(done) == TURN:
            begin = group + PACK - TURN
            staged[:, pl.ds(begin, TURN), :] = jnp.swapaxes(jnp.stack(done), 0, 1)
            done = []

    step_rows = 8
    total = jnp.zeros((block, columns), jnp.float32)
    for start in range(0, outputs, step_rows):
        value = staged[pl.ds(start, step_rows)]
        rounded = value.astype(jnp.bfloat16)
        high[pl.ds(start, step_rows)] = rounded
        low[pl.ds(start, step_rows)] = (value - rounded.astype(jnp.float32)).astype(jnp.bfloat16)
        total = total + jnp.sum(value * value, axis=0)
    power[...] = total


def smooth(half_widths, mask, centre, sides, caps, spans, row_band, col_band, block=32):
    channels, tile_rows, columns = centre.shape
    outputs = mask.shape[0]
    per_turn = LANES // block
    whole = lambda shape: pl.BlockSpec(shape, lambda i: (0,) * len(shape))
    halo = lambda x: pl.BlockSpec(x.shape[:2] + (LANES,), lambda i: (0, 0, i // per_turn))
    split_spec = pl.BlockSpec((outputs, block, columns), lambda i: (0, i, 0))
    split_shape = jax.ShapeDtypeStruct((outputs, channels, columns), jnp.bfloat16)
    tables = [mask, row_band, col_band]
    scratch = [
        pltpu.VMEM((outputs, block, columns), jnp.float32),
        pltpu.VMEM((LANES, 2 * HALF, tile_rows), jnp.bfloat16),
    ]
    if caps:
        scratch += [
            pltpu.VMEM((LANES, 2 * HALF, columns), jnp.bfloat16),
            pltpu.VMEM((LANES, 2 * HALF, 2 * HALF), jnp.bfloat16),
        ]
    return pl.pallas_call(
        functools.partial(smooth_kernel, spans, bool(caps)),
        grid=(channels // block,),
        in_specs=[pl.BlockSpec(memory_space=pltpu.SMEM)]
        + [whole(t.shape) for t in tables]
        + [pl.BlockSpec((block, tile_rows, columns), lambda i: (i, 0, 0))]
        + [halo(x) for x in sides + caps],
        out_specs=[split_spec, split_spec, pl.BlockSpec((block, columns), lambda i: (i, 0))],
        out_shape=[
            split_shape,
            split_shape,
            jax.ShapeDtypeStruct((channels, columns), jnp.float32),
        ],
        scratch_shapes=scratch,
        compiler_params=pltpu.CompilerParams(vmem_limit_bytes=VMEM_LIMIT),
        cost_estimate=pl.CostEstimate(
            flops=16 * channels * tile_rows * columns * 256,
            bytes_accessed=80_000_000,
            transcendentals=0,
        ),
        name="smooth",
    )(half_widths, *tables, centre, *sides, *caps)


def delay_kernel(matrix, high, low, out, staged):
    rows = high.shape[0]
    count, _, columns = out.shape
    done = []
    for pair in range(rows // 2):
        first, second = 2 * pair, 2 * pair + 1
        coarse = jnp.concatenate([high[first], high[second]], axis=1)
        fine = jnp.concatenate([low[first], low[second]], axis=1)
        both = jnp.dot(matrix[...], coarse, preferred_element_type=jnp.float32)
        value = both[:count] + both[count:]
        value = value + jnp.dot(matrix[:count], fine, preferred_element_type=jnp.float32)
        done += [value[:, :columns], value[:, columns:]]
        if len(done) == TURN:
            begin = second + 1 - TURN
            staged[:, pl.ds(begin, TURN), :] = jnp.swapaxes(jnp.stack(done), 0, 1)
            done = []
    out[...] = staged[...].astype(jnp.bfloat16)


def delay_chunk(matrix, high, low, block=16):
    rows, channels, columns = high.shape
    count = matrix.shape[0] // 2
    spec = pl.BlockSpec((block, channels, columns), lambda i: (i, 0, 0))
    return pl.pallas_call(
        delay_kernel,
        grid=(rows // block,),
        in_specs=[pl.BlockSpec(matrix.shape, lambda i: (0, 0)), spec, spec],
        out_specs=pl.BlockSpec((count, block, columns), lambda i: (0, i, 0)),
        out_shape=jax.ShapeDtypeStruct((count, rows, columns), jnp.bfloat16),
        scratch_shapes=[pltpu.VMEM((count, block, columns), jnp.float32)],
        compiler_params=pltpu.CompilerParams(vmem_limit_bytes=VMEM_LIMIT),
        cost_estimate=pl.CostEstimate(
            flops=6 * count * channels * rows * columns,
            bytes_accessed=(4 * channels + 2 * count) * rows * columns,
            transcendentals=0,
        ),
        name="delays",
    )(matrix, high, low)


def correct_kernel(weights, delays, modes, out):
    _, count, rows, _ = delays.shape
    mode_count = modes.shape[1]

    @pl.loop(0, rows // HALF)
    def _(part):
        here = pl.ds(pl.multiple_of(part * HALF, HALF), HALF)
        values = [modes[0, m, here].astype(jnp.float32) for m in range(mode_count)]
        for d in range(count):
            total = delays[0, d, here].astype(jnp.float32)
            for m in range(mode_count):
                total = total - weights[d, m] * values[m]
            out[0, d, here] = total.astype(jnp.bfloat16)


def correct(weights, delays, modes):
    peers = delays.shape[0]
    piece = lambda x: pl.BlockSpec((1,) + x.shape[1:], lambda i: (i, 0, 0, 0))
    return pl.pallas_call(
        correct_kernel,
        grid=(peers,),
        in_specs=[pl.BlockSpec(memory_space=pltpu.SMEM), piece(delays), piece(modes)],
        out_specs=piece(delays),
        out_shape=jax.ShapeDtypeStruct(delays.shape, delays.dtype),
        compiler_params=pltpu.CompilerParams(vmem_limit_bytes=VMEM_LIMIT),
        cost_estimate=pl.CostEstimate(
            flops=32 * delays.size, bytes_accessed=4 * delays.size, transcendentals=0
        ),
        name="correct",
    )(weights, delays, modes)


def spatial_kernel(row_count, col_count, head, tail, col_table, row_table, *refs):
    out, halfway = refs[-2:]
    tile_rows = head.shape[2] + tail.shape[2]
    side = row_count * tile_rows
    for a in range(row_count):
        line = jnp.concatenate(
            [
                jnp.concatenate(
                    [slab[a * col_count + b, k] for k in range(2) for b in range(col_count)], axis=1
                )
                for slab in (head, tail)
            ],
            axis=0,
        )
        part = jnp.dot(line, col_table[...], preferred_element_type=jnp.float32)
        part = part.astype(jnp.bfloat16)
        columns = part.shape[1] // 2
        halfway[pl.ds(a * tile_rows, tile_rows), :] = part[:, :columns]
        halfway[pl.ds(side + a * tile_rows, tile_rows), :] = part[:, columns:]
    step = side // 2
    for k in range(2):
        for s in range(side // step):
            rows = row_table[pl.ds(k * side + s * step, step), :]
            out[0, k, pl.ds(s * step, step), :] = jnp.dot(
                rows, halfway[...], preferred_element_type=jnp.float32
            )


def spatial_chunk(head, tail, col_table, row_table, shape, start, previous):
    peers, parts, tail_rows, tile_cols = tail.shape
    items, head_rows = parts // 2, head.shape[2]
    side, columns = shape[2], shape[3]
    row_count, col_count = side // (head_rows + tail_rows), columns // tile_cols
    in_specs = [
        pl.BlockSpec((peers, 2, head_rows, tile_cols), lambda i: (0, start + i, 0, 0)),
        pl.BlockSpec((peers, 2, tail_rows, tile_cols), lambda i: (0, i, 0, 0)),
        pl.BlockSpec(col_table.shape, lambda i: (0, 0)),
        pl.BlockSpec(row_table.shape, lambda i: (0, 0)),
    ]
    operands = [head, tail, col_table, row_table]
    aliases = {}
    if previous is not None:
        in_specs.append(pl.BlockSpec(memory_space=pl.ANY))
        operands.append(previous)
        aliases = {4: 0}
    return pl.pallas_call(
        functools.partial(spatial_kernel, row_count, col_count),
        grid=(items,),
        in_specs=in_specs,
        out_specs=pl.BlockSpec((1, 2, side, columns), lambda i: (start + i, 0, 0, 0)),
        out_shape=jax.ShapeDtypeStruct(shape, jnp.float32),
        scratch_shapes=[pltpu.VMEM((2 * side, columns), jnp.bfloat16)],
        input_output_aliases=aliases,
        compiler_params=pltpu.CompilerParams(vmem_limit_bytes=VMEM_LIMIT),
        cost_estimate=pl.CostEstimate(
            flops=16 * items * side * side * columns,
            bytes_accessed=items * 12 * side * columns,
            transcendentals=0,
        ),
        name="spatial",
    )(*operands)


def pinned(x):
    return with_layout_constraint(x, Layout(major_to_minor=tuple(range(x.ndim))))


def shifted(x, axis, step):
    size = lax.axis_size(axis)
    pairs = [(i, i + step) for i in range(size) if 0 <= i + step < size]
    return pinned(lax.ppermute(pinned(x), axis, pairs))


def outside(length):
    return [*range(-HALF, 0), *range(length, length + HALF)]


def exact_dot(x, y):
    return jnp.dot(x, y, precision=highest, preferred_element_type=jnp.float32)


def fit(normal_matrix, modes):
    factor = jnp.linalg.cholesky(normal_matrix)
    return jax.scipy.linalg.cho_solve((factor, True), modes)


def split_high_low(x):
    rounded = lax.reduce_precision(x, exponent_bits=8, mantissa_bits=7)
    return rounded.astype(jnp.bfloat16), (x - rounded).astype(jnp.bfloat16)


def chunk_sizes(per_device):
    if per_device <= 4 * END_DELAYS:
        return [per_device]
    return [per_device - END_DELAYS, END_DELAYS]


def tiled_body(sky_cube, half_widths, pixel_mask, foreground_modes):
    tile_rows, tile_cols, channels = sky_cube.shape
    row_count, col_count = lax.axis_size("row"), lax.axis_size("col")
    peers = row_count * col_count
    per_device = channels // 2 // peers
    sides, columns = row_count * tile_rows, col_count * tile_cols

    sky_cube, last, initial = lax.optimization_barrier((sky_cube, sky_cube[LAST], sky_cube[FIRST]))
    top, bottom = shifted(last, "row", 1), shifted(initial, "row", -1)
    left, right = shifted(sky_cube[:, LAST], "col", 1), shifted(sky_cube[:, FIRST], "col", -1)
    centre = jnp.transpose(sky_cube, (2, 0, 1))
    left, right, centre = lax.optimization_barrier((left, right, centre))
    ends = [jnp.concatenate([left[rows], right[rows]], axis=1) for rows in (LAST, FIRST)]
    top_ends, bottom_ends = shifted(ends[0], "row", 1), shifted(ends[1], "row", -1)

    narrow = band_table(range(tile_cols), [*range(tile_cols), *outside(tile_cols)])
    narrow = np.swapaxes(narrow, 1, 2)
    col_band = np.zeros((HALF, PACK, tile_cols + PACK * 2 * HALF, tile_cols), narrow.dtype)
    col_band[:, :, :tile_cols] = narrow[:, None, :tile_cols]
    for member in range(PACK):
        begin = tile_cols + member * 2 * HALF
        col_band[:, member, begin : begin + 2 * HALF] = narrow[:, tile_cols:]
    col_band = col_band.reshape((HALF * PACK,) + col_band.shape[2:])
    mask = pixel_mask.astype(jnp.float32)

    head_end = HALF + HEAD_ROWS
    head_rows = list(range(HALF, head_end))
    tail_rows = [*range(HALF), *range(head_end, tile_rows)]
    head_span = ((0, head_end + HALF),)
    tail_spans = ((0, 2 * HALF), (HEAD_ROWS, tile_rows))

    modes_t = foreground_modes.T
    delay_table = delay_rows(channels, peers, [per_device])
    mode_delays = exact_dot(delay_table, modes_t)
    plain_fit = fit(exact_dot(foreground_modes, modes_t), foreground_modes)

    def stacked(matrix, begin, end):
        matrix = matrix.reshape(peers, per_device, 2, channels)[:, begin:end]
        return jnp.concatenate(split_high_low(matrix.reshape(-1, channels)), axis=0)

    def exchange(delays, items):
        delays = delays.reshape(peers, 2 * items, -1, tile_cols)
        return lax.all_to_all(delays, ("row", "col"), split_axis=0, concat_axis=0, tiled=True)

    head_high, head_low, head_power = smooth(
        half_widths,
        mask[HALF:head_end],
        centre,
        [left, right],
        [],
        head_span,
        band_table(head_rows, range(head_span[0][1])),
        col_band,
    )
    plain = stacked(delay_table - exact_dot(mode_delays, plain_fit), 0, per_device)
    head_delays = delay_chunk(plain, head_high, head_low)
    head = exchange(head_delays, per_device)

    _, top = lax.optimization_barrier((head_delays, top))
    tail_in = [r for a, b in tail_spans for r in range(a, b)] + outside(tile_rows)
    tail_high, tail_low, tail_power = smooth(
        half_widths,
        jnp.concatenate([mask[:HALF], mask[head_end:]], axis=0),
        centre,
        [left, right],
        [top, bottom, top_ends, bottom_ends],
        tail_spans,
        band_table(tail_rows, tail_in),
        col_band,
    )

    power_sum = lax.psum(jnp.sum(head_power + tail_power, axis=1), ("row", "col"))
    weights = 1.0 / (power_sum / (sides * columns) + 1e-05)
    channel_weights = weights / jnp.mean(weights)
    weighted_modes = foreground_modes * weights[None, :]
    weighted_fit = fit(exact_dot(weighted_modes, modes_t), weighted_modes)
    change = jnp.concatenate(split_high_low(weighted_fit - plain_fit), axis=0)
    amplitude = delay_chunk(change, head_high, head_low)
    amplitude = lax.all_gather(amplitude, ("row", "col"), axis=0, tiled=False)
    matrix = delay_table - exact_dot(mode_delays, weighted_fit)

    place = lax.axis_index("row") * col_count + lax.axis_index("col")
    own = lax.dynamic_slice_in_dim(mode_delays, place * 2 * per_device, 2 * per_device, axis=0)
    head = correct(own, head, amplitude)

    cos_c, sin_c = dft_parts(columns)
    col_table = np.block([[cos_c, sin_c], [-sin_c, cos_c]])
    cos_r, sin_r = dft_parts(sides)
    order = [a * tile_rows + r for a in range(row_count) for r in head_rows + tail_rows]
    cos_r, sin_r = cos_r[:, order], sin_r[:, order]
    row_table = np.block([[cos_r, -sin_r], [sin_r, cos_r]])

    shape = (per_device, 2, sides, columns)
    spectrum = None
    start = 0
    for size in chunk_sizes(per_device):
        delays = delay_chunk(stacked(matrix, start, start + size), tail_high, tail_low)
        tail = exchange(delays, size)
        spectrum = spatial_chunk(head, tail, col_table, row_table, shape, start, spectrum)
        start += size
    return (spectrum, channel_weights)


def small_tile_body(sky_cube, half_widths, pixel_mask, foreground_modes):
    tile_rows, tile_cols, channels = sky_cube.shape
    row_count, col_count = lax.axis_size("row"), lax.axis_size("col")
    peers = row_count * col_count
    per_device = channels // 2 // peers
    sides, columns = row_count * tile_rows, col_count * tile_cols
    beam_taps = make_taps(half_widths)
    extended = padded(sky_cube, (("row", 0),), HALF)
    row_part = jnp.einsum(
        "oif,icf->ocf",
        banded_taps(tile_rows, beam_taps),
        extended,
        preferred_element_type=jnp.float32,
    ).astype(jnp.bfloat16)
    row_smoothed = padded(row_part, (("col", 1),), HALF)
    smoothed = jnp.einsum(
        "oif,rif->rof",
        banded_taps(tile_cols, beam_taps),
        row_smoothed,
        preferred_element_type=jnp.float32,
    )
    masked = pixel_mask.astype(jnp.float32)[:, :, None] * smoothed
    pixels = masked.reshape(tile_rows * tile_cols, channels)
    power_sum = lax.psum(jnp.sum(masked * masked, axis=(0, 1)), ("row", "col"))
    weights = 1.0 / (power_sum / (sides * columns) + 1e-05)
    channel_weights = weights / jnp.mean(weights)
    weighted_modes = foreground_modes * weights[None, :]
    normal_matrix = jnp.dot(
        weighted_modes, foreground_modes.T, precision=highest, preferred_element_type=jnp.float32
    )
    projected = jnp.dot(
        pixels, weighted_modes.T, precision=highest, preferred_element_type=jnp.float32
    )
    factor = jnp.linalg.cholesky(normal_matrix)
    amplitude = jax.scipy.linalg.cho_solve((factor, True), projected.T)
    cleaned = pixels - jnp.dot(
        amplitude.T, foreground_modes, precision=highest, preferred_element_type=jnp.float32
    )
    delay_tile = lax.dot_general(
        delay_rows(channels, peers, [per_device]),
        cleaned,
        (((1,), (1,)), ((), ())),
        precision=highest,
        preferred_element_type=jnp.float32,
    )
    sendable = delay_tile.astype(jnp.bfloat16).reshape(
        peers, per_device, 2, tile_rows, tile_cols
    )
    regrouped = lax.all_to_all(sendable, ("row", "col"), split_axis=0, concat_axis=0, tiled=True)
    slab = regrouped.reshape(row_count, col_count, per_device, 2, tile_rows, tile_cols)
    slab = slab.transpose(2, 3, 0, 4, 1, 5).reshape(per_device, 2, sides, columns)
    cos_c, sin_c = dft_parts(columns)
    col_table = np.stack([np.stack([cos_c, -sin_c]), np.stack([sin_c, cos_c])])
    cos_r, sin_r = dft_parts(sides)
    row_table = np.stack([np.stack([cos_r, -sin_r]), np.stack([sin_r, cos_r])])
    halfway = jnp.einsum(
        "kmrc,nmcd->knrd", slab, col_table, preferred_element_type=jnp.float32
    ).astype(jnp.bfloat16)
    spectrum = jnp.einsum(
        "nmsr,kmrd->knsd", row_table, halfway, preferred_element_type=jnp.float32
    )
    return (spectrum, channel_weights)


def body(sky_cube, half_widths, pixel_mask, foreground_modes):
    tile_rows, tile_cols, channels = sky_cube.shape
    fits = tile_rows % 128 == 0 and tile_cols % 128 == 0 and channels % 128 == 0
    run = tiled_body if fits else small_tile_body
    return run(sky_cube, half_widths, pixel_mask, foreground_modes)


def solution(mesh):
    return jax.shard_map(
        body,
        mesh=mesh,
        in_specs=(P(("grp", "row"), "col", None), P(), P(("grp", "row"), "col"), P("grp", None)),
        out_specs=(P(("grp", "row", "col"), None, None, None), P("grp")),
        check_vma=False,
    )
```

```python
import functools
import math

import jax
import jax.numpy as jnp
import numpy as np
from jax import lax
from jax.experimental import pallas as pl
from jax.experimental.layout import Layout, with_layout_constraint
from jax.experimental.pallas import tpu as pltpu
from jax.sharding import PartitionSpec as P

HALF = 16
VMEM_LIMIT = 48 * 1024 * 1024
PACK = 4
TURN = 8
HEAD_ROWS = 48
LANES = 128
FIRST, LAST = slice(0, HALF), slice(-HALF, None)
END_DELAYS = 2

highest = lax.Precision.HIGHEST


def padded(x, sides, width):
    for axis, dim in sides:
        size, length = (lax.axis_size(axis), x.shape[dim])
        up = [(i, (i + 1) % size) for i in range(size - 1)]
        down = [(j, i) for i, j in up]
        last = lax.slice_in_dim(x, length - width, length, axis=dim)
        initial = lax.slice_in_dim(x, 0, width, axis=dim)
        before = lax.ppermute(last, axis, up)
        after = lax.ppermute(initial, axis, down)
        x = jnp.concatenate([before, x, after], axis=dim)
    return x


def make_taps(half_widths):
    offsets = jnp.arange(2 * HALF + 1, dtype=jnp.int32) - HALF
    distance = offsets.astype(jnp.float32)[:, None]
    spread = half_widths.astype(jnp.float32)[None, :] * 0.5
    inside = jnp.abs(offsets)[:, None] <= half_widths[None, :]
    profile = jnp.where(
        inside, jnp.exp(-distance * distance / (2.0 * spread * spread)), jnp.float32(0.0)
    )
    return (profile / jnp.sum(profile, axis=0, keepdims=True)).astype(jnp.bfloat16)


def banded_taps(outputs, beam_taps):
    offsets = (
        jnp.arange(outputs + 2 * HALF, dtype=jnp.int32)[None, :]
        - jnp.arange(outputs, dtype=jnp.int32)[:, None]
    )
    one_hot = (
        offsets[:, :, None] == jnp.arange(2 * HALF + 1, dtype=jnp.int32)[None, None, :]
    ).astype(jnp.bfloat16)
    return jnp.einsum("oit,tf->oif", one_hot, beam_taps, preferred_element_type=jnp.float32).astype(
        jnp.bfloat16
    )


def window_taper(length):
    angles = 2.0 * math.pi * np.arange(length) / (length - 1)
    return (
        0.35875
        - 0.48829 * np.cos(angles)
        + 0.14128 * np.cos(2.0 * angles)
        - 0.01168 * np.cos(3.0 * angles)
    )


def dft_parts(length):
    indices = np.arange(length)
    angles = 2.0 * math.pi * (indices[:, None] * indices[None, :] % length) / length
    scale = 1.0 / math.sqrt(length)
    return (
        (np.cos(angles) * scale).astype(jnp.bfloat16),
        (-np.sin(angles) * scale).astype(jnp.bfloat16),
    )


def delay_rows(channels, peers, sizes):
    per_device = channels // 2 // peers
    order, start = [], 0
    for size in sizes:
        for peer in range(peers):
            order.extend(peer * per_device + start + item for item in range(size))
        start += size
    delays = np.asarray(order)
    channel = np.arange(channels)
    angles = 2.0 * math.pi * (delays[:, None] * channel[None, :] % channels) / channels
    rows = np.stack([np.cos(angles), -np.sin(angles)], axis=1).reshape(channels, channels)
    return (rows * (window_taper(channels) / math.sqrt(channels))[None, :]).astype(np.float32)


def tap_table():
    distance = np.arange(HALF + 1, dtype=np.float32)
    table = np.zeros((HALF, HALF + 1), np.float32)
    for width in range(1, HALF + 1):
        spread = np.float32(width) * np.float32(0.5)
        profile = np.exp(-distance * distance / (np.float32(2.0) * spread * spread))
        profile = np.where(distance <= width, profile, np.float32(0.0)).astype(np.float32)
        total = profile[0] + np.float32(2.0) * np.sum(profile[1:], dtype=np.float32)
        table[width - 1] = profile / total
    return table


def band_table(out_places, in_places):
    taps = np.concatenate([tap_table(), np.zeros((HALF, 1), np.float32)], axis=1)
    distance = np.abs(np.asarray(out_places)[:, None] - np.asarray(in_places)[None, :])
    return taps[:, np.minimum(distance, HALF + 1)].astype(jnp.bfloat16)


def smooth_kernel(spans, capped, widths, mask, row_band, col_band, centre, left, right, *refs):
    if capped:
        top, bottom, top_ends, bottom_ends, *refs = refs
        high, low, power, staged, caps, corners = refs
    else:
        high, low, power, staged = refs
    block = centre.shape[0]
    outputs, columns = mask.shape
    rows = left.shape[2]
    step = pl.program_id(0)
    per_turn = LANES // block

    if capped:

        @pl.when(step % per_turn == 0)
        def _():
            caps[:, FIRST] = jnp.transpose(top[...], (2, 0, 1))
            caps[:, HALF : 2 * HALF] = jnp.transpose(bottom[...], (2, 0, 1))
            corners[:, FIRST] = jnp.transpose(top_ends[...], (2, 0, 1))
            corners[:, HALF : 2 * HALF] = jnp.transpose(bottom_ends[...], (2, 0, 1))

    first = step * block
    lane = (step % per_turn) * block
    kept = mask[...]
    done = []
    for group in range(0, block, PACK):
        members = range(group, group + PACK)
        chosen = pl.ds(group, PACK)
        flank = jnp.concatenate([left[chosen], right[chosen]], axis=1)
        flank = flank.reshape(PACK * 2 * HALF, rows).T
        flank = [flank[a:b] for a, b in spans]
        if capped:
            corner = [corners[lane + j] for j in members]
            flank.append(jnp.concatenate(corner, axis=1))
        flank = jnp.concatenate(flank, axis=0)
        half_smoothed = []
        for j in members:
            data = [centre[j, a:b] for a, b in spans]
            if capped:
                data.append(caps[lane + j])
            data = jnp.concatenate([jnp.concatenate(data, axis=0), flank], axis=1)
            band = row_band[widths[first + j] - 1]
            half_smoothed.append(
                jnp.dot(band, data, preferred_element_type=jnp.float32).astype(jnp.bfloat16)
            )
        for j, half in zip(members, half_smoothed):
            band = col_band[(widths[first + j] - 1) * PACK + j % PACK]
            smoothed = jnp.dot(half, band, preferred_element_type=jnp.float32)
            done.append(smoothed * kept)
        if len(done) == TURN:
            begin = group + PACK - TURN
            staged[:, pl.ds(begin, TURN), :] = jnp.swapaxes(jnp.stack(done), 0, 1)
            done = []

    step_rows = 8
    total = jnp.zeros((block, columns), jnp.float32)
    for start in range(0, outputs, step_rows):
        value = staged[pl.ds(start, step_rows)]
        rounded = value.astype(jnp.bfloat16)
        high[pl.ds(start, step_rows)] = rounded
        low[pl.ds(start, step_rows)] = (value - rounded.astype(jnp.float32)).astype(jnp.bfloat16)
        total = total + jnp.sum(value * value, axis=0)
    power[...] = total


def smooth(half_widths, mask, centre, sides, caps, spans, row_band, col_band, block=32):
    channels, tile_rows, columns = centre.shape
    outputs = mask.shape[0]
    per_turn = LANES // block
    whole = lambda shape: pl.BlockSpec(shape, lambda i: (0,) * len(shape))
    halo = lambda x: pl.BlockSpec(x.shape[:2] + (LANES,), lambda i: (0, 0, i // per_turn))
    split_spec = pl.BlockSpec((outputs, block, columns), lambda i: (0, i, 0))
    split_shape = jax.ShapeDtypeStruct((outputs, channels, columns), jnp.bfloat16)
    tables = [mask, row_band, col_band]
    scratch = [pltpu.VMEM((outputs, block, columns), jnp.float32)]
    if caps:
        scratch += [
            pltpu.VMEM((LANES, 2 * HALF, columns), jnp.bfloat16),
            pltpu.VMEM((LANES, 2 * HALF, 2 * HALF), jnp.bfloat16),
        ]
    return pl.pallas_call(
        functools.partial(smooth_kernel, spans, bool(caps)),
        grid=(channels // block,),
        in_specs=[pl.BlockSpec(memory_space=pltpu.SMEM)]
        + [whole(t.shape) for t in tables]
        + [pl.BlockSpec((block,) + x.shape[1:], lambda i: (i, 0, 0)) for x in [centre] + sides]
        + [halo(x) for x in caps],
        out_specs=[split_spec, split_spec, pl.BlockSpec((block, columns), lambda i: (i, 0))],
        out_shape=[
            split_shape,
            split_shape,
            jax.ShapeDtypeStruct((channels, columns), jnp.float32),
        ],
        scratch_shapes=scratch,
        compiler_params=pltpu.CompilerParams(vmem_limit_bytes=VMEM_LIMIT),
        cost_estimate=pl.CostEstimate(
            flops=16 * channels * tile_rows * columns * 256,
            bytes_accessed=80_000_000,
            transcendentals=0,
        ),
        name="smooth",
    )(half_widths, *tables, centre, *sides, *caps)


def delay_kernel(matrix, high, low, out, staged):
    rows = high.shape[0]
    count, _, columns = out.shape
    done = []
    for pair in range(rows // 2):
        first, second = 2 * pair, 2 * pair + 1
        coarse = jnp.concatenate([high[first], high[second]], axis=1)
        fine = jnp.concatenate([low[first], low[second]], axis=1)
        both = jnp.dot(matrix[...], coarse, preferred_element_type=jnp.float32)
        value = both[:count] + both[count:]
        value = value + jnp.dot(matrix[:count], fine, preferred_element_type=jnp.float32)
        done += [value[:, :columns], value[:, columns:]]
        if len(done) == TURN:
            begin = second + 1 - TURN
            staged[:, pl.ds(begin, TURN), :] = jnp.swapaxes(jnp.stack(done), 0, 1)
            done = []
    out[...] = staged[...].astype(jnp.bfloat16)


def delay_chunk(matrix, high, low, block=16):
    rows, channels, columns = high.shape
    count = matrix.shape[0] // 2
    spec = pl.BlockSpec((block, channels, columns), lambda i: (i, 0, 0))
    return pl.pallas_call(
        delay_kernel,
        grid=(rows // block,),
        in_specs=[pl.BlockSpec(matrix.shape, lambda i: (0, 0)), spec, spec],
        out_specs=pl.BlockSpec((count, block, columns), lambda i: (0, i, 0)),
        out_shape=jax.ShapeDtypeStruct((count, rows, columns), jnp.bfloat16),
        scratch_shapes=[pltpu.VMEM((count, block, columns), jnp.float32)],
        compiler_params=pltpu.CompilerParams(vmem_limit_bytes=VMEM_LIMIT),
        cost_estimate=pl.CostEstimate(
            flops=6 * count * channels * rows * columns,
            bytes_accessed=(4 * channels + 2 * count) * rows * columns,
            transcendentals=0,
        ),
        name="delays",
    )(matrix, high, low)


def correct_kernel(weights, delays, modes, out):
    _, count, rows, _ = delays.shape
    mode_count = modes.shape[1]

    @pl.loop(0, rows // HALF)
    def _(part):
        here = pl.ds(pl.multiple_of(part * HALF, HALF), HALF)
        values = [modes[0, m, here].astype(jnp.float32) for m in range(mode_count)]
        for d in range(count):
            total = delays[0, d, here].astype(jnp.float32)
            for m in range(mode_count):
                total = total - weights[d, m] * values[m]
            out[0, d, here] = total.astype(jnp.bfloat16)


def correct(weights, delays, modes):
    peers = delays.shape[0]
    piece = lambda x: pl.BlockSpec((1,) + x.shape[1:], lambda i: (i, 0, 0, 0))
    return pl.pallas_call(
        correct_kernel,
        grid=(peers,),
        in_specs=[pl.BlockSpec(memory_space=pltpu.SMEM), piece(delays), piece(modes)],
        out_specs=piece(delays),
        out_shape=jax.ShapeDtypeStruct(delays.shape, delays.dtype),
        compiler_params=pltpu.CompilerParams(vmem_limit_bytes=VMEM_LIMIT),
        cost_estimate=pl.CostEstimate(
            flops=32 * delays.size, bytes_accessed=4 * delays.size, transcendentals=0
        ),
        name="correct",
    )(weights, delays, modes)


def spatial_kernel(row_count, col_count, head, tail, col_table, row_table, *refs):
    out, halfway = refs[-2:]
    tile_rows = head.shape[2] + tail.shape[2]
    side = row_count * tile_rows
    for a in range(row_count):
        line = jnp.concatenate(
            [
                jnp.concatenate(
                    [slab[a * col_count + b, k] for k in range(2) for b in range(col_count)], axis=1
                )
                for slab in (head, tail)
            ],
            axis=0,
        )
        part = jnp.dot(line, col_table[...], preferred_element_type=jnp.float32)
        part = part.astype(jnp.bfloat16)
        columns = part.shape[1] // 2
        halfway[pl.ds(a * tile_rows, tile_rows), :] = part[:, :columns]
        halfway[pl.ds(side + a * tile_rows, tile_rows), :] = part[:, columns:]
    step = side // 2
    for k in range(2):
        for s in range(side // step):
            rows = row_table[pl.ds(k * side + s * step, step), :]
            out[0, k, pl.ds(s * step, step), :] = jnp.dot(
                rows, halfway[...], preferred_element_type=jnp.float32
            )


def spatial_chunk(head, tail, col_table, row_table, shape, start, previous):
    peers, parts, tail_rows, tile_cols = tail.shape
    items, head_rows = parts // 2, head.shape[2]
    side, columns = shape[2], shape[3]
    row_count, col_count = side // (head_rows + tail_rows), columns // tile_cols
    in_specs = [
        pl.BlockSpec((peers, 2, head_rows, tile_cols), lambda i: (0, start + i, 0, 0)),
        pl.BlockSpec((peers, 2, tail_rows, tile_cols), lambda i: (0, i, 0, 0)),
        pl.BlockSpec(col_table.shape, lambda i: (0, 0)),
        pl.BlockSpec(row_table.shape, lambda i: (0, 0)),
    ]
    operands = [head, tail, col_table, row_table]
    aliases = {}
    if previous is not None:
        in_specs.append(pl.BlockSpec(memory_space=pl.ANY))
        operands.append(previous)
        aliases = {4: 0}
    return pl.pallas_call(
        functools.partial(spatial_kernel, row_count, col_count),
        grid=(items,),
        in_specs=in_specs,
        out_specs=pl.BlockSpec((1, 2, side, columns), lambda i: (start + i, 0, 0, 0)),
        out_shape=jax.ShapeDtypeStruct(shape, jnp.float32),
        scratch_shapes=[pltpu.VMEM((2 * side, columns), jnp.bfloat16)],
        input_output_aliases=aliases,
        compiler_params=pltpu.CompilerParams(vmem_limit_bytes=VMEM_LIMIT),
        cost_estimate=pl.CostEstimate(
            flops=16 * items * side * side * columns,
            bytes_accessed=items * 12 * side * columns,
            transcendentals=0,
        ),
        name="spatial",
    )(*operands)


def pinned(x):
    return with_layout_constraint(x, Layout(major_to_minor=tuple(range(x.ndim))))


def shifted(x, axis, step):
    size = lax.axis_size(axis)
    pairs = [(i, i + step) for i in range(size) if 0 <= i + step < size]
    return pinned(lax.ppermute(pinned(x), axis, pairs))


def gathered(x):
    shape = x.shape
    bits = 0
    for axis in ("row", "col"):
        size = lax.axis_size(axis)
        for bit in reversed(range(size.bit_length() - 1)):
            other = pinned(lax.ppermute(x, axis, [(i, i ^ (1 << bit)) for i in range(size)]))
            upper = (lax.axis_index(axis) >> bit) % 2 == 1
            pair = [jnp.where(upper, other, x), jnp.where(upper, x, other)]
            x = jnp.stack(pair, axis=bits)
            bits += 1
    return x.reshape((-1,) + shape)


def outside(length):
    return [*range(-HALF, 0), *range(length, length + HALF)]


def exact_dot(x, y):
    return jnp.dot(x, y, precision=highest, preferred_element_type=jnp.float32)


def fit(normal_matrix, modes):
    factor = jnp.linalg.cholesky(normal_matrix)
    return jax.scipy.linalg.cho_solve((factor, True), modes)


def split_high_low(x):
    rounded = lax.reduce_precision(x, exponent_bits=8, mantissa_bits=7)
    return rounded.astype(jnp.bfloat16), (x - rounded).astype(jnp.bfloat16)


def chunk_sizes(per_device):
    if per_device <= 4 * END_DELAYS:
        return [per_device]
    return [per_device - END_DELAYS, END_DELAYS]


def tiled_body(sky_cube, half_widths, pixel_mask, foreground_modes):
    tile_rows, tile_cols, channels = sky_cube.shape
    row_count, col_count = lax.axis_size("row"), lax.axis_size("col")
    peers = row_count * col_count
    per_device = channels // 2 // peers
    sides, columns = row_count * tile_rows, col_count * tile_cols

    sky_cube, last, initial = lax.optimization_barrier((sky_cube, sky_cube[LAST], sky_cube[FIRST]))
    top, bottom = shifted(last, "row", 1), shifted(initial, "row", -1)
    left, right = shifted(sky_cube[:, LAST], "col", 1), shifted(sky_cube[:, FIRST], "col", -1)
    centre = jnp.transpose(sky_cube, (2, 0, 1))
    left, right, centre = lax.optimization_barrier((left, right, centre))
    ends = [jnp.concatenate([left[rows], right[rows]], axis=1) for rows in (LAST, FIRST)]
    top_ends, bottom_ends = shifted(ends[0], "row", 1), shifted(ends[1], "row", -1)

    narrow = band_table(range(tile_cols), [*range(tile_cols), *outside(tile_cols)])
    narrow = np.swapaxes(narrow, 1, 2)
    col_band = np.zeros((HALF, PACK, tile_cols + PACK * 2 * HALF, tile_cols), narrow.dtype)
    col_band[:, :, :tile_cols] = narrow[:, None, :tile_cols]
    for member in range(PACK):
        begin = tile_cols + member * 2 * HALF
        col_band[:, member, begin : begin + 2 * HALF] = narrow[:, tile_cols:]
    col_band = col_band.reshape((HALF * PACK,) + col_band.shape[2:])
    mask = pixel_mask.astype(jnp.float32)

    head_end = HALF + HEAD_ROWS
    head_rows = list(range(HALF, head_end))
    tail_rows = [*range(HALF), *range(head_end, tile_rows)]
    head_span = ((0, head_end + HALF),)
    tail_spans = ((0, 2 * HALF), (HEAD_ROWS, tile_rows))

    sides_t = [jnp.transpose(x, (2, 1, 0)) for x in (left, right)]
    sides_t[0], top, bottom = lax.optimization_barrier((sides_t[0], top, bottom))

    modes_t = foreground_modes.T
    delay_table = delay_rows(channels, peers, [per_device])
    mode_delays = exact_dot(delay_table, modes_t)
    plain_fit = fit(exact_dot(foreground_modes, modes_t), foreground_modes)

    def stacked(matrix, begin, end):
        matrix = matrix.reshape(peers, per_device, 2, channels)[:, begin:end]
        return jnp.concatenate(split_high_low(matrix.reshape(-1, channels)), axis=0)

    def exchange(delays, items):
        delays = delays.reshape(peers, 2 * items, -1, tile_cols)
        return lax.all_to_all(delays, ("row", "col"), split_axis=0, concat_axis=0, tiled=True)

    head_high, head_low, head_power = smooth(
        half_widths,
        mask[HALF:head_end],
        centre,
        sides_t,
        [],
        head_span,
        band_table(head_rows, range(head_span[0][1])),
        col_band,
    )
    plain = stacked(delay_table - exact_dot(mode_delays, plain_fit), 0, per_device)
    head_delays = delay_chunk(plain, head_high, head_low)
    head_delays, *ends = lax.optimization_barrier((head_delays, top_ends, bottom_ends))
    head = exchange(head_delays, per_device)
    top_ends, bottom_ends = ends
    tail_in = [r for a, b in tail_spans for r in range(a, b)] + outside(tile_rows)
    tail_high, tail_low, tail_power = smooth(
        half_widths,
        jnp.concatenate([mask[:HALF], mask[head_end:]], axis=0),
        centre,
        sides_t,
        [top, bottom, top_ends, bottom_ends],
        tail_spans,
        band_table(tail_rows, tail_in),
        col_band,
    )

    power_sum = lax.psum(jnp.sum(head_power + tail_power, axis=1), ("row", "col"))
    weights = 1.0 / (power_sum / (sides * columns) + 1e-05)
    channel_weights = weights / jnp.mean(weights)
    weighted_modes = foreground_modes * weights[None, :]
    weighted_fit = fit(exact_dot(weighted_modes, modes_t), weighted_modes)
    change = jnp.concatenate(split_high_low(weighted_fit - plain_fit), axis=0)
    amplitude = delay_chunk(change, head_high, head_low)
    amplitude = gathered(amplitude)
    matrix = delay_table - exact_dot(mode_delays, weighted_fit)

    place = lax.axis_index("row") * col_count + lax.axis_index("col")
    own = lax.dynamic_slice_in_dim(mode_delays, place * 2 * per_device, 2 * per_device, axis=0)
    head = correct(own, head, amplitude)

    cos_c, sin_c = dft_parts(columns)
    col_table = np.block([[cos_c, sin_c], [-sin_c, cos_c]])
    cos_r, sin_r = dft_parts(sides)
    order = [a * tile_rows + r for a in range(row_count) for r in head_rows + tail_rows]
    cos_r, sin_r = cos_r[:, order], sin_r[:, order]
    row_table = np.block([[cos_r, -sin_r], [sin_r, cos_r]])

    shape = (per_device, 2, sides, columns)
    spectrum = None
    start = 0
    for size in chunk_sizes(per_device):
        delays = delay_chunk(stacked(matrix, start, start + size), tail_high, tail_low)
        tail = exchange(delays, size)
        spectrum = spatial_chunk(head, tail, col_table, row_table, shape, start, spectrum)
        start += size
    return (spectrum, channel_weights)


def small_tile_body(sky_cube, half_widths, pixel_mask, foreground_modes):
    tile_rows, tile_cols, channels = sky_cube.shape
    row_count, col_count = lax.axis_size("row"), lax.axis_size("col")
    peers = row_count * col_count
    per_device = channels // 2 // peers
    sides, columns = row_count * tile_rows, col_count * tile_cols
    beam_taps = make_taps(half_widths)
    extended = padded(sky_cube, (("row", 0),), HALF)
    row_part = jnp.einsum(
        "oif,icf->ocf",
        banded_taps(tile_rows, beam_taps),
        extended,
        preferred_element_type=jnp.float32,
    ).astype(jnp.bfloat16)
    row_smoothed = padded(row_part, (("col", 1),), HALF)
    smoothed = jnp.einsum(
        "oif,rif->rof",
        banded_taps(tile_cols, beam_taps),
        row_smoothed,
        preferred_element_type=jnp.float32,
    )
    masked = pixel_mask.astype(jnp.float32)[:, :, None] * smoothed
    pixels = masked.reshape(tile_rows * tile_cols, channels)
    power_sum = lax.psum(jnp.sum(masked * masked, axis=(0, 1)), ("row", "col"))
    weights = 1.0 / (power_sum / (sides * columns) + 1e-05)
    channel_weights = weights / jnp.mean(weights)
    weighted_modes = foreground_modes * weights[None, :]
    normal_matrix = jnp.dot(
        weighted_modes, foreground_modes.T, precision=highest, preferred_element_type=jnp.float32
    )
    projected = jnp.dot(
        pixels, weighted_modes.T, precision=highest, preferred_element_type=jnp.float32
    )
    factor = jnp.linalg.cholesky(normal_matrix)
    amplitude = jax.scipy.linalg.cho_solve((factor, True), projected.T)
    cleaned = pixels - jnp.dot(
        amplitude.T, foreground_modes, precision=highest, preferred_element_type=jnp.float32
    )
    delay_tile = lax.dot_general(
        delay_rows(channels, peers, [per_device]),
        cleaned,
        (((1,), (1,)), ((), ())),
        precision=highest,
        preferred_element_type=jnp.float32,
    )
    sendable = delay_tile.astype(jnp.bfloat16).reshape(
        peers, per_device, 2, tile_rows, tile_cols
    )
    regrouped = lax.all_to_all(sendable, ("row", "col"), split_axis=0, concat_axis=0, tiled=True)
    slab = regrouped.reshape(row_count, col_count, per_device, 2, tile_rows, tile_cols)
    slab = slab.transpose(2, 3, 0, 4, 1, 5).reshape(per_device, 2, sides, columns)
    cos_c, sin_c = dft_parts(columns)
    col_table = np.stack([np.stack([cos_c, -sin_c]), np.stack([sin_c, cos_c])])
    cos_r, sin_r = dft_parts(sides)
    row_table = np.stack([np.stack([cos_r, -sin_r]), np.stack([sin_r, cos_r])])
    halfway = jnp.einsum(
        "kmrc,nmcd->knrd", slab, col_table, preferred_element_type=jnp.float32
    ).astype(jnp.bfloat16)
    spectrum = jnp.einsum(
        "nmsr,kmrd->knsd", row_table, halfway, preferred_element_type=jnp.float32
    )
    return (spectrum, channel_weights)


def body(sky_cube, half_widths, pixel_mask, foreground_modes):
    tile_rows, tile_cols, channels = sky_cube.shape
    fits = tile_rows % 128 == 0 and tile_cols % 128 == 0 and channels % 128 == 0
    for axis in ("row", "col"):
        fits = fits and lax.axis_size(axis) & (lax.axis_size(axis) - 1) == 0
    run = tiled_body if fits else small_tile_body
    return run(sky_cube, half_widths, pixel_mask, foreground_modes)


def solution(mesh):
    return jax.shard_map(
        body,
        mesh=mesh,
        in_specs=(P(("grp", "row"), "col", None), P(), P(("grp", "row"), "col"), P("grp", None)),
        out_specs=(P(("grp", "row", "col"), None, None, None), P("grp")),
        check_vma=False,
    )
```

```python
import functools
import math

import jax
import jax.numpy as jnp
import numpy as np
from jax import lax
from jax.experimental import pallas as pl
from jax.experimental.layout import Layout, with_layout_constraint
from jax.experimental.pallas import tpu as pltpu
from jax.sharding import PartitionSpec as P

HALF = 16
VMEM_LIMIT = 48 * 1024 * 1024
PACK = 4
TURN = 8
HEAD_ROWS = 16
LANES = 128
FIRST, LAST = slice(0, HALF), slice(-HALF, None)
END_DELAYS = 2

highest = lax.Precision.HIGHEST


def padded(x, sides, width):
    for axis, dim in sides:
        size, length = (lax.axis_size(axis), x.shape[dim])
        up = [(i, (i + 1) % size) for i in range(size - 1)]
        down = [(j, i) for i, j in up]
        last = lax.slice_in_dim(x, length - width, length, axis=dim)
        initial = lax.slice_in_dim(x, 0, width, axis=dim)
        before = lax.ppermute(last, axis, up)
        after = lax.ppermute(initial, axis, down)
        x = jnp.concatenate([before, x, after], axis=dim)
    return x


def make_taps(half_widths):
    offsets = jnp.arange(2 * HALF + 1, dtype=jnp.int32) - HALF
    distance = offsets.astype(jnp.float32)[:, None]
    spread = half_widths.astype(jnp.float32)[None, :] * 0.5
    inside = jnp.abs(offsets)[:, None] <= half_widths[None, :]
    profile = jnp.where(
        inside, jnp.exp(-distance * distance / (2.0 * spread * spread)), jnp.float32(0.0)
    )
    return (profile / jnp.sum(profile, axis=0, keepdims=True)).astype(jnp.bfloat16)


def banded_taps(outputs, beam_taps):
    offsets = (
        jnp.arange(outputs + 2 * HALF, dtype=jnp.int32)[None, :]
        - jnp.arange(outputs, dtype=jnp.int32)[:, None]
    )
    one_hot = (
        offsets[:, :, None] == jnp.arange(2 * HALF + 1, dtype=jnp.int32)[None, None, :]
    ).astype(jnp.bfloat16)
    return jnp.einsum("oit,tf->oif", one_hot, beam_taps, preferred_element_type=jnp.float32).astype(
        jnp.bfloat16
    )


def window_taper(length):
    angles = 2.0 * math.pi * np.arange(length) / (length - 1)
    return (
        0.35875
        - 0.48829 * np.cos(angles)
        + 0.14128 * np.cos(2.0 * angles)
        - 0.01168 * np.cos(3.0 * angles)
    )


def dft_parts(length):
    indices = np.arange(length)
    angles = 2.0 * math.pi * (indices[:, None] * indices[None, :] % length) / length
    scale = 1.0 / math.sqrt(length)
    return (
        (np.cos(angles) * scale).astype(jnp.bfloat16),
        (-np.sin(angles) * scale).astype(jnp.bfloat16),
    )


def delay_rows(channels, peers, sizes):
    per_device = channels // 2 // peers
    order, start = [], 0
    for size in sizes:
        for peer in range(peers):
            order.extend(peer * per_device + start + item for item in range(size))
        start += size
    delays = np.asarray(order)
    channel = np.arange(channels)
    angles = 2.0 * math.pi * (delays[:, None] * channel[None, :] % channels) / channels
    rows = np.stack([np.cos(angles), -np.sin(angles)], axis=1).reshape(channels, channels)
    return (rows * (window_taper(channels) / math.sqrt(channels))[None, :]).astype(np.float32)


def tap_table():
    distance = np.arange(HALF + 1, dtype=np.float32)
    table = np.zeros((HALF, HALF + 1), np.float32)
    for width in range(1, HALF + 1):
        spread = np.float32(width) * np.float32(0.5)
        profile = np.exp(-distance * distance / (np.float32(2.0) * spread * spread))
        profile = np.where(distance <= width, profile, np.float32(0.0)).astype(np.float32)
        total = profile[0] + np.float32(2.0) * np.sum(profile[1:], dtype=np.float32)
        table[width - 1] = profile / total
    return table


def band_table(out_places, in_places):
    taps = np.concatenate([tap_table(), np.zeros((HALF, 1), np.float32)], axis=1)
    distance = np.abs(np.asarray(out_places)[:, None] - np.asarray(in_places)[None, :])
    return taps[:, np.minimum(distance, HALF + 1)].astype(jnp.bfloat16)


def smooth_kernel(spans, capped, widths, mask, row_band, col_band, centre, left, right, *refs):
    if capped:
        top, bottom, top_ends, bottom_ends, *refs = refs
        high, low, power, staged, caps, corners = refs
    else:
        high, low, power, staged = refs
    block = centre.shape[0]
    outputs, columns = mask.shape
    rows = left.shape[2]
    step = pl.program_id(0)
    per_turn = LANES // block

    if capped:

        @pl.when(step % per_turn == 0)
        def _():
            caps[:, FIRST] = jnp.transpose(top[...], (2, 0, 1))
            caps[:, HALF : 2 * HALF] = jnp.transpose(bottom[...], (2, 0, 1))
            corners[:, FIRST] = jnp.transpose(top_ends[...], (2, 0, 1))
            corners[:, HALF : 2 * HALF] = jnp.transpose(bottom_ends[...], (2, 0, 1))

    first = step * block
    lane = (step % per_turn) * block
    kept = mask[...]
    done = []
    for group in range(0, block, PACK):
        members = range(group, group + PACK)
        chosen = pl.ds(group, PACK)
        flank = jnp.concatenate([left[chosen], right[chosen]], axis=1)
        flank = flank.reshape(PACK * 2 * HALF, rows).T
        flank = [flank[a:b] for a, b in spans]
        if capped:
            corner = [corners[lane + j] for j in members]
            flank.append(jnp.concatenate(corner, axis=1))
        flank = jnp.concatenate(flank, axis=0)
        half_smoothed = []
        for j in members:
            data = [centre[j, a:b] for a, b in spans]
            if capped:
                data.append(caps[lane + j])
            data = jnp.concatenate([jnp.concatenate(data, axis=0), flank], axis=1)
            band = row_band[widths[first + j] - 1]
            half_smoothed.append(
                jnp.dot(band, data, preferred_element_type=jnp.float32).astype(jnp.bfloat16)
            )
        for j, half in zip(members, half_smoothed):
            band = col_band[(widths[first + j] - 1) * PACK + j % PACK]
            smoothed = jnp.dot(half, band, preferred_element_type=jnp.float32)
            done.append(smoothed * kept)
        if len(done) == TURN:
            begin = group + PACK - TURN
            staged[:, pl.ds(begin, TURN), :] = jnp.swapaxes(jnp.stack(done), 0, 1)
            done = []

    step_rows = 8
    total = jnp.zeros((block, columns), jnp.float32)
    for start in range(0, outputs, step_rows):
        value = staged[pl.ds(start, step_rows)]
        rounded = value.astype(jnp.bfloat16)
        high[pl.ds(start, step_rows)] = rounded
        low[pl.ds(start, step_rows)] = (value - rounded.astype(jnp.float32)).astype(jnp.bfloat16)
        total = total + jnp.sum(value * value, axis=0)
    power[...] = total


def smooth(half_widths, mask, centre, sides, caps, spans, row_band, col_band, block=32):
    channels, tile_rows, columns = centre.shape
    outputs = mask.shape[0]
    per_turn = LANES // block
    whole = lambda shape: pl.BlockSpec(shape, lambda i: (0,) * len(shape))
    halo = lambda x: pl.BlockSpec(x.shape[:2] + (LANES,), lambda i: (0, 0, i // per_turn))
    split_spec = pl.BlockSpec((outputs, block, columns), lambda i: (0, i, 0))
    split_shape = jax.ShapeDtypeStruct((outputs, channels, columns), jnp.bfloat16)
    tables = [mask, row_band, col_band]
    scratch = [pltpu.VMEM((outputs, block, columns), jnp.float32)]
    if caps:
        scratch += [
            pltpu.VMEM((LANES, 2 * HALF, columns), jnp.bfloat16),
            pltpu.VMEM((LANES, 2 * HALF, 2 * HALF), jnp.bfloat16),
        ]
    return pl.pallas_call(
        functools.partial(smooth_kernel, spans, bool(caps)),
        grid=(channels // block,),
        in_specs=[pl.BlockSpec(memory_space=pltpu.SMEM)]
        + [whole(t.shape) for t in tables]
        + [pl.BlockSpec((block,) + x.shape[1:], lambda i: (i, 0, 0)) for x in [centre] + sides]
        + [halo(x) for x in caps],
        out_specs=[split_spec, split_spec, pl.BlockSpec((block, columns), lambda i: (i, 0))],
        out_shape=[
            split_shape,
            split_shape,
            jax.ShapeDtypeStruct((channels, columns), jnp.float32),
        ],
        scratch_shapes=scratch,
        compiler_params=pltpu.CompilerParams(vmem_limit_bytes=VMEM_LIMIT),
        cost_estimate=pl.CostEstimate(
            flops=16 * channels * tile_rows * columns * 256,
            bytes_accessed=80_000_000,
            transcendentals=0,
        ),
        name="smooth",
    )(half_widths, *tables, centre, *sides, *caps)


def delay_kernel(matrix, high, low, out, staged):
    rows = high.shape[0]
    count, _, columns = out.shape
    done = []
    for pair in range(rows // 2):
        first, second = 2 * pair, 2 * pair + 1
        coarse = jnp.concatenate([high[first], high[second]], axis=1)
        fine = jnp.concatenate([low[first], low[second]], axis=1)
        both = jnp.dot(matrix[...], coarse, preferred_element_type=jnp.float32)
        value = both[:count] + both[count:]
        value = value + jnp.dot(matrix[:count], fine, preferred_element_type=jnp.float32)
        done += [value[:, :columns], value[:, columns:]]
        if len(done) == TURN:
            begin = second + 1 - TURN
            staged[:, pl.ds(begin, TURN), :] = jnp.swapaxes(jnp.stack(done), 0, 1)
            done = []
    out[...] = staged[...].astype(jnp.bfloat16)


def delay_chunk(matrix, high, low, begin, rows, block=16):
    _, channels, columns = high.shape
    count = matrix.shape[0] // 2
    spec = pl.BlockSpec((block, channels, columns), lambda i: (begin // block + i, 0, 0))
    return pl.pallas_call(
        delay_kernel,
        grid=(rows // block,),
        in_specs=[pl.BlockSpec(matrix.shape, lambda i: (0, 0)), spec, spec],
        out_specs=pl.BlockSpec((count, block, columns), lambda i: (0, i, 0)),
        out_shape=jax.ShapeDtypeStruct((count, rows, columns), jnp.bfloat16),
        scratch_shapes=[pltpu.VMEM((count, block, columns), jnp.float32)],
        compiler_params=pltpu.CompilerParams(vmem_limit_bytes=VMEM_LIMIT),
        cost_estimate=pl.CostEstimate(
            flops=6 * count * channels * rows * columns,
            bytes_accessed=(4 * channels + 2 * count) * rows * columns,
            transcendentals=0,
        ),
        name="delays",
    )(matrix, high, low)


def spatial_kernel(row_count, col_count, head, tail, col_table, row_table, *refs):
    out, halfway = refs[-2:]
    tile_rows = head.shape[2] + tail.shape[2]
    side = row_count * tile_rows
    for a in range(row_count):
        line = jnp.concatenate(
            [
                jnp.concatenate(
                    [slab[a * col_count + b, k] for k in range(2) for b in range(col_count)], axis=1
                )
                for slab in (head, tail)
            ],
            axis=0,
        )
        part = jnp.dot(line, col_table[...], preferred_element_type=jnp.float32)
        part = part.astype(jnp.bfloat16)
        columns = part.shape[1] // 2
        halfway[pl.ds(a * tile_rows, tile_rows), :] = part[:, :columns]
        halfway[pl.ds(side + a * tile_rows, tile_rows), :] = part[:, columns:]
    step = side // 2
    for k in range(2):
        for s in range(side // step):
            rows = row_table[pl.ds(k * side + s * step, step), :]
            out[0, k, pl.ds(s * step, step), :] = jnp.dot(
                rows, halfway[...], preferred_element_type=jnp.float32
            )


def spatial_chunk(head, tail, col_table, row_table, shape, start, previous):
    peers, parts, tail_rows, tile_cols = tail.shape
    items, head_rows = parts // 2, head.shape[2]
    side, columns = shape[2], shape[3]
    row_count, col_count = side // (head_rows + tail_rows), columns // tile_cols
    in_specs = [
        pl.BlockSpec((peers, 2, head_rows, tile_cols), lambda i: (0, start + i, 0, 0)),
        pl.BlockSpec((peers, 2, tail_rows, tile_cols), lambda i: (0, i, 0, 0)),
        pl.BlockSpec(col_table.shape, lambda i: (0, 0)),
        pl.BlockSpec(row_table.shape, lambda i: (0, 0)),
    ]
    operands = [head, tail, col_table, row_table]
    aliases = {}
    if previous is not None:
        in_specs.append(pl.BlockSpec(memory_space=pl.ANY))
        operands.append(previous)
        aliases = {4: 0}
    return pl.pallas_call(
        functools.partial(spatial_kernel, row_count, col_count),
        grid=(items,),
        in_specs=in_specs,
        out_specs=pl.BlockSpec((1, 2, side, columns), lambda i: (start + i, 0, 0, 0)),
        out_shape=jax.ShapeDtypeStruct(shape, jnp.float32),
        scratch_shapes=[pltpu.VMEM((2 * side, columns), jnp.bfloat16)],
        input_output_aliases=aliases,
        compiler_params=pltpu.CompilerParams(vmem_limit_bytes=VMEM_LIMIT),
        cost_estimate=pl.CostEstimate(
            flops=16 * items * side * side * columns,
            bytes_accessed=items * 12 * side * columns,
            transcendentals=0,
        ),
        name="spatial",
    )(*operands)


def pinned(x):
    return with_layout_constraint(x, Layout(major_to_minor=tuple(range(x.ndim))))


def shifted(x, axis, step):
    size = lax.axis_size(axis)
    pairs = [(i, i + step) for i in range(size) if 0 <= i + step < size]
    return pinned(lax.ppermute(pinned(x), axis, pairs))


def outside(length):
    return [*range(-HALF, 0), *range(length, length + HALF)]


def exact_dot(x, y):
    return jnp.dot(x, y, precision=highest, preferred_element_type=jnp.float32)


def fit(normal_matrix, modes):
    factor = jnp.linalg.cholesky(normal_matrix)
    return jax.scipy.linalg.cho_solve((factor, True), modes)


def split_high_low(x):
    rounded = lax.reduce_precision(x, exponent_bits=8, mantissa_bits=7)
    return rounded.astype(jnp.bfloat16), (x - rounded).astype(jnp.bfloat16)


def chunk_sizes(per_device):
    if per_device <= 4 * END_DELAYS:
        return [per_device]
    return [per_device - END_DELAYS, END_DELAYS]


def tiled_body(sky_cube, half_widths, pixel_mask, foreground_modes):
    tile_rows, tile_cols, channels = sky_cube.shape
    row_count, col_count = lax.axis_size("row"), lax.axis_size("col")
    peers = row_count * col_count
    per_device = channels // 2 // peers
    sides, columns = row_count * tile_rows, col_count * tile_cols

    sky_cube, last, initial = lax.optimization_barrier((sky_cube, sky_cube[LAST], sky_cube[FIRST]))
    top, bottom = shifted(last, "row", 1), shifted(initial, "row", -1)
    left, right = shifted(sky_cube[:, LAST], "col", 1), shifted(sky_cube[:, FIRST], "col", -1)
    centre = jnp.transpose(sky_cube, (2, 0, 1))
    left, right, centre = lax.optimization_barrier((left, right, centre))
    ends = [jnp.concatenate([left[rows], right[rows]], axis=1) for rows in (LAST, FIRST)]
    top_ends, bottom_ends = shifted(ends[0], "row", 1), shifted(ends[1], "row", -1)

    narrow = band_table(range(tile_cols), [*range(tile_cols), *outside(tile_cols)])
    narrow = np.swapaxes(narrow, 1, 2)
    col_band = np.zeros((HALF, PACK, tile_cols + PACK * 2 * HALF, tile_cols), narrow.dtype)
    col_band[:, :, :tile_cols] = narrow[:, None, :tile_cols]
    for member in range(PACK):
        begin = tile_cols + member * 2 * HALF
        col_band[:, member, begin : begin + 2 * HALF] = narrow[:, tile_cols:]
    col_band = col_band.reshape((HALF * PACK,) + col_band.shape[2:])
    high, low, power = smooth(
        half_widths,
        pixel_mask.astype(jnp.float32),
        centre,
        [jnp.transpose(x, (2, 1, 0)) for x in (left, right)],
        [top, bottom, top_ends, bottom_ends],
        ((0, tile_rows),),
        band_table(range(tile_rows), [*range(tile_rows), *outside(tile_rows)]),
        col_band,
    )

    def exchange(x):
        return lax.all_to_all(x, ("row", "col"), split_axis=0, concat_axis=0, tiled=True)

    modes_t = foreground_modes.T
    delay_table = delay_rows(channels, peers, [per_device])
    mode_delays = exact_dot(delay_table, modes_t)
    tile_power = jnp.broadcast_to(jnp.sum(power, axis=1)[None], (peers, channels))
    power_sum = jnp.sum(exchange(tile_power), axis=0)
    weights = 1.0 / (power_sum / (sides * columns) + 1e-05)
    channel_weights = weights / jnp.mean(weights)
    weighted_modes = foreground_modes * weights[None, :]
    weighted_fit = fit(exact_dot(weighted_modes, modes_t), weighted_modes)
    matrix = split_high_low(delay_table - exact_dot(mode_delays, weighted_fit))

    def send(begin, end, first_row, rows):
        parts = [
            x.reshape(peers, per_device, 2, channels)[:, begin:end].reshape(-1, channels)
            for x in matrix
        ]
        delays = delay_chunk(jnp.concatenate(parts, axis=0), high, low, first_row, rows)
        return exchange(delays.reshape(peers, 2 * (end - begin), rows, tile_cols))

    cos_c, sin_c = dft_parts(columns)
    col_table = np.block([[cos_c, sin_c], [-sin_c, cos_c]])
    cos_r, sin_r = dft_parts(sides)
    row_table = np.block([[cos_r, -sin_r], [sin_r, cos_r]])

    shape = (per_device, 2, sides, columns)
    head = send(0, per_device, 0, HEAD_ROWS)
    spectrum = None
    start = 0
    for size in chunk_sizes(per_device):
        tail = send(start, start + size, HEAD_ROWS, tile_rows - HEAD_ROWS)
        spectrum = spatial_chunk(head, tail, col_table, row_table, shape, start, spectrum)
        start += size
    return (spectrum, channel_weights)


def small_tile_body(sky_cube, half_widths, pixel_mask, foreground_modes):
    tile_rows, tile_cols, channels = sky_cube.shape
    row_count, col_count = lax.axis_size("row"), lax.axis_size("col")
    peers = row_count * col_count
    per_device = channels // 2 // peers
    sides, columns = row_count * tile_rows, col_count * tile_cols
    beam_taps = make_taps(half_widths)
    extended = padded(sky_cube, (("row", 0),), HALF)
    row_part = jnp.einsum(
        "oif,icf->ocf",
        banded_taps(tile_rows, beam_taps),
        extended,
        preferred_element_type=jnp.float32,
    ).astype(jnp.bfloat16)
    row_smoothed = padded(row_part, (("col", 1),), HALF)
    smoothed = jnp.einsum(
        "oif,rif->rof",
        banded_taps(tile_cols, beam_taps),
        row_smoothed,
        preferred_element_type=jnp.float32,
    )
    masked = pixel_mask.astype(jnp.float32)[:, :, None] * smoothed
    pixels = masked.reshape(tile_rows * tile_cols, channels)
    power_sum = lax.psum(jnp.sum(masked * masked, axis=(0, 1)), ("row", "col"))
    weights = 1.0 / (power_sum / (sides * columns) + 1e-05)
    channel_weights = weights / jnp.mean(weights)
    weighted_modes = foreground_modes * weights[None, :]
    normal_matrix = jnp.dot(
        weighted_modes, foreground_modes.T, precision=highest, preferred_element_type=jnp.float32
    )
    projected = jnp.dot(
        pixels, weighted_modes.T, precision=highest, preferred_element_type=jnp.float32
    )
    factor = jnp.linalg.cholesky(normal_matrix)
    amplitude = jax.scipy.linalg.cho_solve((factor, True), projected.T)
    cleaned = pixels - jnp.dot(
        amplitude.T, foreground_modes, precision=highest, preferred_element_type=jnp.float32
    )
    delay_tile = lax.dot_general(
        delay_rows(channels, peers, [per_device]),
        cleaned,
        (((1,), (1,)), ((), ())),
        precision=highest,
        preferred_element_type=jnp.float32,
    )
    sendable = delay_tile.astype(jnp.bfloat16).reshape(
        peers, per_device, 2, tile_rows, tile_cols
    )
    regrouped = lax.all_to_all(sendable, ("row", "col"), split_axis=0, concat_axis=0, tiled=True)
    slab = regrouped.reshape(row_count, col_count, per_device, 2, tile_rows, tile_cols)
    slab = slab.transpose(2, 3, 0, 4, 1, 5).reshape(per_device, 2, sides, columns)
    cos_c, sin_c = dft_parts(columns)
    col_table = np.stack([np.stack([cos_c, -sin_c]), np.stack([sin_c, cos_c])])
    cos_r, sin_r = dft_parts(sides)
    row_table = np.stack([np.stack([cos_r, -sin_r]), np.stack([sin_r, cos_r])])
    halfway = jnp.einsum(
        "kmrc,nmcd->knrd", slab, col_table, preferred_element_type=jnp.float32
    ).astype(jnp.bfloat16)
    spectrum = jnp.einsum(
        "nmsr,kmrd->knsd", row_table, halfway, preferred_element_type=jnp.float32
    )
    return (spectrum, channel_weights)


def body(sky_cube, half_widths, pixel_mask, foreground_modes):
    tile_rows, tile_cols, channels = sky_cube.shape
    fits = tile_rows % 128 == 0 and tile_cols % 128 == 0 and channels % 128 == 0
    run = tiled_body if fits else small_tile_body
    return run(sky_cube, half_widths, pixel_mask, foreground_modes)


def solution(mesh):
    return jax.shard_map(
        body,
        mesh=mesh,
        in_specs=(P(("grp", "row"), "col", None), P(), P(("grp", "row"), "col"), P("grp", None)),
        out_specs=(P(("grp", "row", "col"), None, None, None), P("grp")),
        check_vma=False,
    )
```

```python
import functools
import math

import jax
import jax.numpy as jnp
import numpy as np
from jax import lax
from jax.experimental import pallas as pl
from jax.experimental.layout import Layout, with_layout_constraint
from jax.experimental.pallas import tpu as pltpu
from jax.sharding import PartitionSpec as P

HALF = 16
VMEM_LIMIT = 48 * 1024 * 1024
PACK = 4
TURN = 8
HEAD_ROWS = 16
LANES = 128
FIRST, LAST = slice(0, HALF), slice(-HALF, None)
END_DELAYS = 2

highest = lax.Precision.HIGHEST


def padded(x, sides, width):
    for axis, dim in sides:
        size, length = (lax.axis_size(axis), x.shape[dim])
        up = [(i, (i + 1) % size) for i in range(size - 1)]
        down = [(j, i) for i, j in up]
        last = lax.slice_in_dim(x, length - width, length, axis=dim)
        initial = lax.slice_in_dim(x, 0, width, axis=dim)
        before = lax.ppermute(last, axis, up)
        after = lax.ppermute(initial, axis, down)
        x = jnp.concatenate([before, x, after], axis=dim)
    return x


def make_taps(half_widths):
    offsets = jnp.arange(2 * HALF + 1, dtype=jnp.int32) - HALF
    distance = offsets.astype(jnp.float32)[:, None]
    spread = half_widths.astype(jnp.float32)[None, :] * 0.5
    inside = jnp.abs(offsets)[:, None] <= half_widths[None, :]
    profile = jnp.where(
        inside, jnp.exp(-distance * distance / (2.0 * spread * spread)), jnp.float32(0.0)
    )
    return (profile / jnp.sum(profile, axis=0, keepdims=True)).astype(jnp.bfloat16)


def banded_taps(outputs, beam_taps):
    offsets = (
        jnp.arange(outputs + 2 * HALF, dtype=jnp.int32)[None, :]
        - jnp.arange(outputs, dtype=jnp.int32)[:, None]
    )
    one_hot = (
        offsets[:, :, None] == jnp.arange(2 * HALF + 1, dtype=jnp.int32)[None, None, :]
    ).astype(jnp.bfloat16)
    return jnp.einsum("oit,tf->oif", one_hot, beam_taps, preferred_element_type=jnp.float32).astype(
        jnp.bfloat16
    )


def window_taper(length):
    angles = 2.0 * math.pi * np.arange(length) / (length - 1)
    return (
        0.35875
        - 0.48829 * np.cos(angles)
        + 0.14128 * np.cos(2.0 * angles)
        - 0.01168 * np.cos(3.0 * angles)
    )


def dft_parts(length):
    indices = np.arange(length)
    angles = 2.0 * math.pi * (indices[:, None] * indices[None, :] % length) / length
    scale = 1.0 / math.sqrt(length)
    return (
        (np.cos(angles) * scale).astype(jnp.bfloat16),
        (-np.sin(angles) * scale).astype(jnp.bfloat16),
    )


def delay_rows(channels, peers, sizes):
    per_device = channels // 2 // peers
    order, start = [], 0
    for size in sizes:
        for peer in range(peers):
            order.extend(peer * per_device + start + item for item in range(size))
        start += size
    delays = np.asarray(order)
    channel = np.arange(channels)
    angles = 2.0 * math.pi * (delays[:, None] * channel[None, :] % channels) / channels
    rows = np.stack([np.cos(angles), -np.sin(angles)], axis=1).reshape(channels, channels)
    return (rows * (window_taper(channels) / math.sqrt(channels))[None, :]).astype(np.float32)


def tap_table():
    distance = np.arange(HALF + 1, dtype=np.float32)
    table = np.zeros((HALF, HALF + 1), np.float32)
    for width in range(1, HALF + 1):
        spread = np.float32(width) * np.float32(0.5)
        profile = np.exp(-distance * distance / (np.float32(2.0) * spread * spread))
        profile = np.where(distance <= width, profile, np.float32(0.0)).astype(np.float32)
        total = profile[0] + np.float32(2.0) * np.sum(profile[1:], dtype=np.float32)
        table[width - 1] = profile / total
    return table


def band_table(out_places, in_places):
    taps = np.concatenate([tap_table(), np.zeros((HALF, 1), np.float32)], axis=1)
    distance = np.abs(np.asarray(out_places)[:, None] - np.asarray(in_places)[None, :])
    return taps[:, np.minimum(distance, HALF + 1)].astype(jnp.bfloat16)


def smooth_kernel(spans, capped, widths, mask, row_band, col_band, centre, left, right, *refs):
    if capped:
        top, bottom, top_ends, bottom_ends, *refs = refs
        high, low, power, staged, caps, corners = refs
    else:
        high, low, power, staged = refs
    block = centre.shape[0]
    outputs, columns = mask.shape
    rows = left.shape[2]
    step = pl.program_id(0)
    per_turn = LANES // block

    if capped:

        @pl.when(step % per_turn == 0)
        def _():
            caps[:, FIRST] = jnp.transpose(top[...], (2, 0, 1))
            caps[:, HALF : 2 * HALF] = jnp.transpose(bottom[...], (2, 0, 1))
            corners[:, FIRST] = jnp.transpose(top_ends[...], (2, 0, 1))
            corners[:, HALF : 2 * HALF] = jnp.transpose(bottom_ends[...], (2, 0, 1))

    first = step * block
    lane = (step % per_turn) * block
    kept = mask[...]
    done = []
    for group in range(0, block, PACK):
        members = range(group, group + PACK)
        chosen = pl.ds(group, PACK)
        flank = jnp.concatenate([left[chosen], right[chosen]], axis=1)
        flank = flank.reshape(PACK * 2 * HALF, rows).T
        flank = [flank[a:b] for a, b in spans]
        if capped:
            corner = [corners[lane + j] for j in members]
            flank.append(jnp.concatenate(corner, axis=1))
        flank = jnp.concatenate(flank, axis=0)
        half_smoothed = []
        for j in members:
            data = [centre[j, a:b] for a, b in spans]
            if capped:
                data.append(caps[lane + j])
            data = jnp.concatenate([jnp.concatenate(data, axis=0), flank], axis=1)
            band = row_band[widths[first + j] - 1]
            half_smoothed.append(
                jnp.dot(band, data, preferred_element_type=jnp.float32).astype(jnp.bfloat16)
            )
        for j, half in zip(members, half_smoothed):
            band = col_band[(widths[first + j] - 1) * PACK + j % PACK]
            smoothed = jnp.dot(half, band, preferred_element_type=jnp.float32)
            done.append(smoothed * kept)
        if len(done) == TURN:
            begin = group + PACK - TURN
            staged[:, pl.ds(begin, TURN), :] = jnp.swapaxes(jnp.stack(done), 0, 1)
            done = []

    step_rows = 8
    total = jnp.zeros((block, columns), jnp.float32)
    for start in range(0, outputs, step_rows):
        value = staged[pl.ds(start, step_rows)]
        rounded = value.astype(jnp.bfloat16)
        high[pl.ds(start, step_rows)] = rounded
        low[pl.ds(start, step_rows)] = (value - rounded.astype(jnp.float32)).astype(jnp.bfloat16)
        total = total + jnp.sum(value * value, axis=0)
    power[...] = total


def smooth(half_widths, mask, centre, sides, caps, spans, row_band, col_band, block=32):
    channels, tile_rows, columns = centre.shape
    outputs = mask.shape[0]
    per_turn = LANES // block
    whole = lambda shape: pl.BlockSpec(shape, lambda i: (0,) * len(shape))
    halo = lambda x: pl.BlockSpec(x.shape[:2] + (LANES,), lambda i: (0, 0, i // per_turn))
    split_spec = pl.BlockSpec((outputs, block, columns), lambda i: (0, i, 0))
    split_shape = jax.ShapeDtypeStruct((outputs, channels, columns), jnp.bfloat16)
    tables = [mask, row_band, col_band]
    scratch = [pltpu.VMEM((outputs, block, columns), jnp.float32)]
    if caps:
        scratch += [
            pltpu.VMEM((LANES, 2 * HALF, columns), jnp.bfloat16),
            pltpu.VMEM((LANES, 2 * HALF, 2 * HALF), jnp.bfloat16),
        ]
    return pl.pallas_call(
        functools.partial(smooth_kernel, spans, bool(caps)),
        grid=(channels // block,),
        in_specs=[pl.BlockSpec(memory_space=pltpu.SMEM)]
        + [whole(t.shape) for t in tables]
        + [pl.BlockSpec((block,) + x.shape[1:], lambda i: (i, 0, 0)) for x in [centre] + sides]
        + [halo(x) for x in caps],
        out_specs=[split_spec, split_spec, pl.BlockSpec((block, columns), lambda i: (i, 0))],
        out_shape=[
            split_shape,
            split_shape,
            jax.ShapeDtypeStruct((channels, columns), jnp.float32),
        ],
        scratch_shapes=scratch,
        compiler_params=pltpu.CompilerParams(vmem_limit_bytes=VMEM_LIMIT),
        cost_estimate=pl.CostEstimate(
            flops=16 * channels * tile_rows * columns * 256,
            bytes_accessed=80_000_000,
            transcendentals=0,
        ),
        name="smooth",
    )(half_widths, *tables, centre, *sides, *caps)


def delay_kernel(matrix, high, low, out, staged):
    rows = high.shape[0]
    count, _, columns = out.shape
    done = []
    for pair in range(rows // 2):
        first, second = 2 * pair, 2 * pair + 1
        coarse = jnp.concatenate([high[first], high[second]], axis=1)
        fine = jnp.concatenate([low[first], low[second]], axis=1)
        both = jnp.dot(matrix[...], coarse, preferred_element_type=jnp.float32)
        value = both[:count] + both[count:]
        value = value + jnp.dot(matrix[:count], fine, preferred_element_type=jnp.float32)
        done += [value[:, :columns], value[:, columns:]]
        if len(done) == TURN:
            begin = second + 1 - TURN
            staged[:, pl.ds(begin, TURN), :] = jnp.swapaxes(jnp.stack(done), 0, 1)
            done = []
    out[...] = staged[...].astype(jnp.bfloat16)


def delay_chunk(matrix, high, low, begin, rows, block=16):
    _, channels, columns = high.shape
    count = matrix.shape[0] // 2
    spec = pl.BlockSpec((block, channels, columns), lambda i: (begin // block + i, 0, 0))
    return pl.pallas_call(
        delay_kernel,
        grid=(rows // block,),
        in_specs=[pl.BlockSpec(matrix.shape, lambda i: (0, 0)), spec, spec],
        out_specs=pl.BlockSpec((count, block, columns), lambda i: (0, i, 0)),
        out_shape=jax.ShapeDtypeStruct((count, rows, columns), jnp.bfloat16),
        scratch_shapes=[pltpu.VMEM((count, block, columns), jnp.float32)],
        compiler_params=pltpu.CompilerParams(vmem_limit_bytes=VMEM_LIMIT),
        cost_estimate=pl.CostEstimate(
            flops=6 * count * channels * rows * columns,
            bytes_accessed=(4 * channels + 2 * count) * rows * columns,
            transcendentals=0,
        ),
        name="delays",
    )(matrix, high, low)


def spatial_kernel(row_count, col_count, head, tail, col_table, row_table, *refs):
    out, halfway = refs[-2:]
    tile_rows = head.shape[2] + tail.shape[2]
    side = row_count * tile_rows
    for a in range(row_count):
        line = jnp.concatenate(
            [
                jnp.concatenate(
                    [slab[a * col_count + b, k] for k in range(2) for b in range(col_count)], axis=1
                )
                for slab in (head, tail)
            ],
            axis=0,
        )
        part = jnp.dot(line, col_table[...], preferred_element_type=jnp.float32)
        part = part.astype(jnp.bfloat16)
        columns = part.shape[1] // 2
        halfway[pl.ds(a * tile_rows, tile_rows), :] = part[:, :columns]
        halfway[pl.ds(side + a * tile_rows, tile_rows), :] = part[:, columns:]
    step = side // 2
    for k in range(2):
        for s in range(side // step):
            rows = row_table[pl.ds(k * side + s * step, step), :]
            out[0, k, pl.ds(s * step, step), :] = jnp.dot(
                rows, halfway[...], preferred_element_type=jnp.float32
            )


def spatial_chunk(head, tail, col_table, row_table, shape, start, previous):
    peers, parts, tail_rows, tile_cols = tail.shape
    items, head_rows = parts // 2, head.shape[2]
    side, columns = shape[2], shape[3]
    row_count, col_count = side // (head_rows + tail_rows), columns // tile_cols
    in_specs = [
        pl.BlockSpec((peers, 2, head_rows, tile_cols), lambda i: (0, start + i, 0, 0)),
        pl.BlockSpec((peers, 2, tail_rows, tile_cols), lambda i: (0, i, 0, 0)),
        pl.BlockSpec(col_table.shape, lambda i: (0, 0)),
        pl.BlockSpec(row_table.shape, lambda i: (0, 0)),
    ]
    operands = [head, tail, col_table, row_table]
    aliases = {}
    if previous is not None:
        in_specs.append(pl.BlockSpec(memory_space=pl.ANY))
        operands.append(previous)
        aliases = {4: 0}
    return pl.pallas_call(
        functools.partial(spatial_kernel, row_count, col_count),
        grid=(items,),
        in_specs=in_specs,
        out_specs=pl.BlockSpec((1, 2, side, columns), lambda i: (start + i, 0, 0, 0)),
        out_shape=jax.ShapeDtypeStruct(shape, jnp.float32),
        scratch_shapes=[pltpu.VMEM((2 * side, columns), jnp.bfloat16)],
        input_output_aliases=aliases,
        compiler_params=pltpu.CompilerParams(vmem_limit_bytes=VMEM_LIMIT),
        cost_estimate=pl.CostEstimate(
            flops=16 * items * side * side * columns,
            bytes_accessed=items * 12 * side * columns,
            transcendentals=0,
        ),
        name="spatial",
    )(*operands)


def pinned(x):
    return with_layout_constraint(x, Layout(major_to_minor=tuple(range(x.ndim))))


def shifted(x, axis, step):
    size = lax.axis_size(axis)
    pairs = [(i, i + step) for i in range(size) if 0 <= i + step < size]
    return pinned(lax.ppermute(pinned(x), axis, pairs))


def outside(length):
    return [*range(-HALF, 0), *range(length, length + HALF)]


def exact_dot(x, y):
    return jnp.dot(x, y, precision=highest, preferred_element_type=jnp.float32)


def fit(normal_matrix, modes):
    factor = jnp.linalg.cholesky(normal_matrix)
    return jax.scipy.linalg.cho_solve((factor, True), modes)


def split_high_low(x):
    rounded = lax.reduce_precision(x, exponent_bits=8, mantissa_bits=7)
    return rounded.astype(jnp.bfloat16), (x - rounded).astype(jnp.bfloat16)


def exchange_by_pairs(x):
    rows, cols = lax.axis_size("row"), lax.axis_size("col")
    place = lax.axis_index("row") * cols + lax.axis_index("col")
    far = [k for k in range(1, rows * cols) if k // cols >= rows // 2]
    near = [k for k in range(1, rows * cols) if k // cols < rows // 2]
    order = [k for pair in zip(far, near) for k in pair] + far[len(near) :]
    brought = []
    for k in order:
        piece = lax.dynamic_slice_in_dim(x, place ^ k, 1, axis=0)
        pairs = [(i, i ^ k) for i in range(rows * cols)]
        brought.append(lax.ppermute(piece, ("row", "col"), pairs))
    for k, piece in zip(order, brought):
        x = lax.dynamic_update_slice_in_dim(x, piece, place ^ k, axis=0)
    return x, brought[-4]


def tiled_body(sky_cube, half_widths, pixel_mask, foreground_modes):
    tile_rows, tile_cols, channels = sky_cube.shape
    row_count, col_count = lax.axis_size("row"), lax.axis_size("col")
    peers = row_count * col_count
    per_device = channels // 2 // peers
    sides, columns = row_count * tile_rows, col_count * tile_cols

    sky_cube, last, initial = lax.optimization_barrier((sky_cube, sky_cube[LAST], sky_cube[FIRST]))
    top, bottom = shifted(last, "row", 1), shifted(initial, "row", -1)
    left, right = shifted(sky_cube[:, LAST], "col", 1), shifted(sky_cube[:, FIRST], "col", -1)
    centre = jnp.transpose(sky_cube, (2, 0, 1))
    left, right, centre, top, bottom = lax.optimization_barrier((left, right, centre, top, bottom))
    ends = [jnp.concatenate([left[rows], right[rows]], axis=1) for rows in (LAST, FIRST)]
    top_ends, bottom_ends = shifted(ends[0], "row", 1), shifted(ends[1], "row", -1)

    narrow = band_table(range(tile_cols), [*range(tile_cols), *outside(tile_cols)])
    narrow = np.swapaxes(narrow, 1, 2)
    col_band = np.zeros((HALF, PACK, tile_cols + PACK * 2 * HALF, tile_cols), narrow.dtype)
    col_band[:, :, :tile_cols] = narrow[:, None, :tile_cols]
    for member in range(PACK):
        begin = tile_cols + member * 2 * HALF
        col_band[:, member, begin : begin + 2 * HALF] = narrow[:, tile_cols:]
    col_band = col_band.reshape((HALF * PACK,) + col_band.shape[2:])
    high, low, power = smooth(
        half_widths,
        pixel_mask.astype(jnp.float32),
        centre,
        [jnp.transpose(x, (2, 1, 0)) for x in (left, right)],
        [top, bottom, top_ends, bottom_ends],
        ((0, tile_rows),),
        band_table(range(tile_rows), [*range(tile_rows), *outside(tile_rows)]),
        col_band,
    )

    def exchange(x):
        return lax.all_to_all(x, ("row", "col"), split_axis=0, concat_axis=0, tiled=True)

    modes_t = foreground_modes.T
    delay_table = delay_rows(channels, peers, [per_device])
    mode_delays = exact_dot(delay_table, modes_t)
    tile_power = jnp.broadcast_to(jnp.sum(power, axis=1)[None], (peers, channels))
    power_sum = jnp.sum(exchange(tile_power), axis=0)
    weights = 1.0 / (power_sum / (sides * columns) + 1e-05)
    channel_weights = weights / jnp.mean(weights)
    weighted_modes = foreground_modes * weights[None, :]
    weighted_fit = fit(exact_dot(weighted_modes, modes_t), weighted_modes)
    matrix = split_high_low(delay_table - exact_dot(mode_delays, weighted_fit))

    def delays(begin, end, first_row, rows):
        parts = [
            x.reshape(peers, per_device, 2, channels)[:, begin:end].reshape(-1, channels)
            for x in matrix
        ]
        part = delay_chunk(jnp.concatenate(parts, axis=0), high, low, first_row, rows)
        return part.reshape(peers, 2 * (end - begin), rows, tile_cols)

    cos_c, sin_c = dft_parts(columns)
    col_table = np.block([[cos_c, sin_c], [-sin_c, cos_c]])
    cos_r, sin_r = dft_parts(sides)
    row_table = np.block([[cos_r, -sin_r], [sin_r, cos_r]])

    shape = (per_device, 2, sides, columns)
    rest = tile_rows - HEAD_ROWS
    split = per_device - END_DELAYS
    head = exchange(delays(0, per_device, 0, HEAD_ROWS))
    middle, near_end = exchange_by_pairs(delays(0, split, HEAD_ROWS, rest))
    last = delays(split, per_device, HEAD_ROWS, rest)
    last, _ = lax.optimization_barrier((last, near_end))
    last = exchange(last)
    spectrum = spatial_chunk(head, middle, col_table, row_table, shape, 0, None)
    spectrum = spatial_chunk(head, last, col_table, row_table, shape, split, spectrum)
    return (spectrum, channel_weights)


def small_tile_body(sky_cube, half_widths, pixel_mask, foreground_modes):
    tile_rows, tile_cols, channels = sky_cube.shape
    row_count, col_count = lax.axis_size("row"), lax.axis_size("col")
    peers = row_count * col_count
    per_device = channels // 2 // peers
    sides, columns = row_count * tile_rows, col_count * tile_cols
    beam_taps = make_taps(half_widths)
    extended = padded(sky_cube, (("row", 0),), HALF)
    row_part = jnp.einsum(
        "oif,icf->ocf",
        banded_taps(tile_rows, beam_taps),
        extended,
        preferred_element_type=jnp.float32,
    ).astype(jnp.bfloat16)
    row_smoothed = padded(row_part, (("col", 1),), HALF)
    smoothed = jnp.einsum(
        "oif,rif->rof",
        banded_taps(tile_cols, beam_taps),
        row_smoothed,
        preferred_element_type=jnp.float32,
    )
    masked = pixel_mask.astype(jnp.float32)[:, :, None] * smoothed
    pixels = masked.reshape(tile_rows * tile_cols, channels)
    power_sum = lax.psum(jnp.sum(masked * masked, axis=(0, 1)), ("row", "col"))
    weights = 1.0 / (power_sum / (sides * columns) + 1e-05)
    channel_weights = weights / jnp.mean(weights)
    weighted_modes = foreground_modes * weights[None, :]
    normal_matrix = jnp.dot(
        weighted_modes, foreground_modes.T, precision=highest, preferred_element_type=jnp.float32
    )
    projected = jnp.dot(
        pixels, weighted_modes.T, precision=highest, preferred_element_type=jnp.float32
    )
    factor = jnp.linalg.cholesky(normal_matrix)
    amplitude = jax.scipy.linalg.cho_solve((factor, True), projected.T)
    cleaned = pixels - jnp.dot(
        amplitude.T, foreground_modes, precision=highest, preferred_element_type=jnp.float32
    )
    delay_tile = lax.dot_general(
        delay_rows(channels, peers, [per_device]),
        cleaned,
        (((1,), (1,)), ((), ())),
        precision=highest,
        preferred_element_type=jnp.float32,
    )
    sendable = delay_tile.astype(jnp.bfloat16).reshape(
        peers, per_device, 2, tile_rows, tile_cols
    )
    regrouped = lax.all_to_all(sendable, ("row", "col"), split_axis=0, concat_axis=0, tiled=True)
    slab = regrouped.reshape(row_count, col_count, per_device, 2, tile_rows, tile_cols)
    slab = slab.transpose(2, 3, 0, 4, 1, 5).reshape(per_device, 2, sides, columns)
    cos_c, sin_c = dft_parts(columns)
    col_table = np.stack([np.stack([cos_c, -sin_c]), np.stack([sin_c, cos_c])])
    cos_r, sin_r = dft_parts(sides)
    row_table = np.stack([np.stack([cos_r, -sin_r]), np.stack([sin_r, cos_r])])
    halfway = jnp.einsum(
        "kmrc,nmcd->knrd", slab, col_table, preferred_element_type=jnp.float32
    ).astype(jnp.bfloat16)
    spectrum = jnp.einsum(
        "nmsr,kmrd->knsd", row_table, halfway, preferred_element_type=jnp.float32
    )
    return (spectrum, channel_weights)


def body(sky_cube, half_widths, pixel_mask, foreground_modes):
    tile_rows, tile_cols, channels = sky_cube.shape
    fits = tile_rows % 128 == 0 and tile_cols % 128 == 0 and channels % 128 == 0
    for axis in ("row", "col"):
        fits = fits and lax.axis_size(axis) & (lax.axis_size(axis) - 1) == 0
    run = tiled_body if fits else small_tile_body
    return run(sky_cube, half_widths, pixel_mask, foreground_modes)


def solution(mesh):
    return jax.shard_map(
        body,
        mesh=mesh,
        in_specs=(P(("grp", "row"), "col", None), P(), P(("grp", "row"), "col"), P("grp", None)),
        out_specs=(P(("grp", "row", "col"), None, None, None), P("grp")),
        check_vma=False,
    )
```
